128 devices in a mesh: row: 64 (over y, x, z), col: 2 (over core).
Axes of the slice: x: 4, y: 4, z: 4, core: 2. Of those that a mesh axis runs over, the one named last changes fastest.
Arguments:
- pair_rep: bfloat16 [2048, 256, 128], P('row', 'col'), may hold values from -6 to 6
- token_counts: int32 [16], replicated, may hold values from 64 to 256, as said below
- first_device: int32 [16], replicated, may hold values from 0 to 62, as said below
- norm_gain: float32 [2, 2, 128], replicated, may hold values from 0.1 to 1.9
- norm_bias: float32 [2, 2, 128], replicated, may hold values from -3 to 3
- proj_weight: bfloat16 [2, 128, 512], replicated, may hold values from -0.5 to 0.5
- gate_weight: bfloat16 [2, 128, 128], replicated, may hold values from -0.5 to 0.5
- out_weight: bfloat16 [2, 128, 128], replicated, may hold values from -0.5 to 0.5
Outputs:
- updated: bfloat16 [2048, 256, 128], P('row', 'col')
The draws below stay inside these ranges and needn't reach their ends.
Inputs may be any that keep to these rules, and one draw needn't show every extreme that they name: Each complex occupies token_counts / 32 consecutive row devices, from 2 to 8; the complexes fill the row axis end to end in order. `first_device`: the sum of the earlier complexes' token counts divided by 32.
All inputs are finite; a program needn't handle non-finite values.
Results may differ from the reference program's by a relative error of at most 0.0065.
Values may be sent and summed in bfloat16 or wider, within the bound.
A program may use at most 128 MiB of HBM per device.

```python
import jax
import jax.numpy as jnp
from jax import lax

CHANNELS = 128
ROWS_DEV = 32
G_MAX = 8
MAXN = 256
COMPLEXES = 16
ROWS_ALL = 2048


def complex_devices(key):
    groups = COMPLEXES // 4
    patterns = jnp.array([[8, 2, 3, 3], [6, 2, 4, 4], [5, 5, 3, 3], [4, 4, 4, 4], [7, 3, 2, 4]], jnp.int32)
    which = jax.random.randint(jax.random.fold_in(key, 11), (groups,), 0, 5)
    which = which.at[0].set(0)
    group_keys = jax.random.split(jax.random.fold_in(key, 12), groups)
    orders = jax.vmap(lambda sub_key: jax.random.permutation(sub_key, 4))(group_keys)
    counts = jnp.take_along_axis(patterns[which], orders, axis=1)
    last_order = jax.random.permutation(jax.random.fold_in(key, 13), 3)
    last_group = jnp.concatenate([jnp.array([8, 3, 3], jnp.int32)[last_order], jnp.array([2], jnp.int32)])
    counts = counts.at[groups - 1].set(last_group)
    return counts.reshape(-1).astype(jnp.int32)


def draw_token_counts(key, part):
    devices = complex_devices(key)
    return (devices * ROWS_DEV).astype(jnp.int32)


def draw_first_device(key, part):
    devices = complex_devices(key)
    return (jnp.cumsum(devices) - devices).astype(jnp.int32)


def block_scale(key, dims, pieces, low, largest):
    def one(dim, blocks):
        draws = jax.random.uniform(jax.random.fold_in(jax.random.fold_in(key, 6), dim), (blocks,), jnp.float32, low / len(pieces), largest / len(pieces))
        return jnp.repeat(jnp.exp(draws), dims[dim] // blocks).reshape((-1,) + (1,) * (len(dims) - dim - 1))

    level = one(*pieces[0])
    for cut in pieces[1:]:
        level = level * one(*cut)
    return level


def normal_values(stream_key, dims, spread, most, shards=(), kind=jnp.bfloat16):
    entries = spread * jax.random.normal(stream_key, dims, jnp.float32)
    if shards:
        entries = entries * block_scale(stream_key, dims, shards, -0.22, 0.18)
    return jnp.clip(entries, -most, most).astype(kind)


def setup_inputs(seed: int = 0) -> dict:
    seeds = jax.random.split(jax.random.key(seed), 9)
    return {
        "pair_rep": normal_values(seeds[0], (ROWS_ALL, MAXN, CHANNELS), 1.0, 6.0, ((0, 64), (1, 2))),
        "token_counts": draw_token_counts(jax.random.fold_in(seeds[8], 71), 0),
        "first_device": draw_first_device(jax.random.fold_in(seeds[8], 71), 0),
        "norm_gain": jnp.clip(1.0 + 0.18 * jax.random.normal(seeds[3], (2, 2, CHANNELS), jnp.float32), 0.1, 1.9),
        "norm_bias": normal_values(seeds[4], (2, 2, CHANNELS), 0.5, 3.0, (), jnp.float32),
        "proj_weight": normal_values(seeds[5], (2, CHANNELS, 4 * CHANNELS), CHANNELS ** -0.5, 0.5),
        "gate_weight": normal_values(seeds[6], (2, CHANNELS, CHANNELS), CHANNELS ** -0.5, 0.5),
        "out_weight": normal_values(seeds[7], (2, CHANNELS, CHANNELS), CHANNELS ** -0.5, 0.5),
    }


EPS = 1e-05

def layer_norm(values, scale_mul, shift_add):
    average = lax.optimization_barrier(jnp.mean(values, axis=-1, keepdims=True))
    centred = values - average
    variance = lax.optimization_barrier(jnp.mean(centred * centred, axis=-1, keepdims=True))
    return centred * lax.rsqrt(variance + EPS) * scale_mul + shift_add

def to_tokens(layout):
    extent = layout.shape[0]
    shaped = layout.reshape(extent, 2, G_MAX, ROWS_DEV // 2, CHANNELS)
    return shaped.transpose(0, 2, 1, 3, 4).reshape(extent, MAXN, CHANNELS)

def from_tokens(ordered):
    extent = ordered.shape[0]
    shaped = ordered.reshape(extent, G_MAX, 2, ROWS_DEV // 2, CHANNELS)
    return shaped.transpose(0, 2, 1, 3, 4).reshape(extent, MAXN, CHANNELS)

def tri_layer(z_bf, inside, layer_no, norm_gain, norm_bias, proj_weight, gate_weight, out_weight):
    side = z_bf.shape[0]
    z_float = z_bf.astype(jnp.float32)
    z_normed = layer_norm(z_float, norm_gain[layer_no, 0], norm_bias[layer_no, 0]).astype(jnp.bfloat16)
    flat = z_normed.reshape(-1, CHANNELS)
    projected = jnp.dot(flat, proj_weight[layer_no], preferred_element_type=jnp.float32)
    projected = projected.reshape(side, side, 4 * CHANNELS)
    left_side = (jax.nn.sigmoid(projected[..., :CHANNELS]) * projected[..., CHANNELS:2 * CHANNELS] * inside).astype(jnp.bfloat16)
    right_side = (jax.nn.sigmoid(projected[..., 2 * CHANNELS:3 * CHANNELS]) * projected[..., 3 * CHANNELS:] * inside).astype(jnp.bfloat16)
    gating = jax.nn.sigmoid(jnp.dot(flat, gate_weight[layer_no], preferred_element_type=jnp.float32)).reshape(side, side, CHANNELS)
    if layer_no == 0:
        summed = jnp.einsum('ikc,jkc->ijc', left_side.astype(jnp.float32), right_side.astype(jnp.float32))
    else:
        summed = jnp.einsum('kic,kjc->ijc', left_side.astype(jnp.float32), right_side.astype(jnp.float32))
    normed_sum = layer_norm(summed, norm_gain[layer_no, 1], norm_bias[layer_no, 1]).astype(jnp.bfloat16)
    update = jnp.dot(normed_sum.reshape(-1, CHANNELS), out_weight[layer_no], preferred_element_type=jnp.float32)
    update = update.reshape(side, side, CHANNELS)
    return ((z_float + gating * update) * inside).astype(jnp.bfloat16)

def reference(pair_rep, token_counts, first_device, norm_gain, norm_bias, proj_weight, gate_weight, out_weight):
    ordered = to_tokens(pair_rep)
    padded = jnp.concatenate([ordered, jnp.zeros((MAXN, MAXN, CHANNELS), jnp.bfloat16)], 0)

    def per_complex(carried, complex_no):
        count_now = token_counts[complex_no]
        first_row = (first_device[complex_no] * ROWS_DEV).astype(jnp.int32)
        sub_block = lax.dynamic_slice_in_dim(padded, first_row, MAXN, 0)
        inside_tok = (jnp.arange(MAXN) < count_now).astype(jnp.float32)
        inside = (inside_tok[:, None] * inside_tok[None, :])[:, :, None]
        after_out = tri_layer(sub_block, inside, 0, norm_gain, norm_bias, proj_weight, gate_weight, out_weight)
        after_in = tri_layer(after_out, inside, 1, norm_gain, norm_bias, proj_weight, gate_weight, out_weight)
        current = lax.dynamic_slice_in_dim(carried, first_row, MAXN, 0)
        carried = lax.dynamic_update_slice_in_dim(carried, current + after_in, first_row, 0)
        return (carried, None)
    start_acc = jnp.zeros((ROWS_ALL + MAXN, MAXN, CHANNELS), jnp.bfloat16)
    finished, unused = lax.scan(per_complex, start_acc, jnp.arange(COMPLEXES, dtype=jnp.int32))
    return from_tokens(finished[:ROWS_ALL])
```

```python
import functools

import jax
import jax.numpy as jnp
from jax import lax
from jax.experimental import pallas as pl
from jax.experimental.pallas import tpu as pltpu
from jax.sharding import PartitionSpec as P

EPS = 1e-05
CH = 128
ROWS = 32
HALF = 16
SPAN = 8
COMPLEXES = 16
DEV_ROWS = 64
DEVS = 128
F32 = jnp.float32
BF16 = jnp.bfloat16
MESH = pl.DeviceIdType.MESH


def sigmoid(x):
    return 0.5 * jnp.tanh(0.5 * x) + 0.5


def flip(x):
    eye = (
        lax.broadcasted_iota(jnp.int32, (CH, CH), 0) == lax.broadcasted_iota(jnp.int32, (CH, CH), 1)
    ).astype(F32).astype(BF16)
    return lax.dot_general(eye, x, (((1,), (1,)), ((), ())), preferred_element_type=F32)


def norm(x, gain, bias):
    average = jnp.sum(x, axis=0, keepdims=True) * (1.0 / CH)
    centred = x - average
    variance = jnp.sum(centred * centred, axis=0, keepdims=True) * (1.0 / CH)
    return (centred * lax.rsqrt(variance + EPS) * gain + bias).astype(BF16)


def prepare(gain_ref, bias_ref, proj_ref, gate_ref, out_ref, wt, wo, gb):
    for layer in range(2):
        for blk in range(4):
            part = slice(blk * CH, (blk + 1) * CH)
            wt[layer, part] = flip(proj_ref[layer, :, part]).astype(BF16)
        wt[layer, 4 * CH :] = flip(gate_ref[layer]).astype(BF16)
        wo[layer] = flip(out_ref[layer]).astype(BF16)
        for which in range(2):
            for kind, ref in enumerate((gain_ref, bias_ref)):
                line = ref[layer, pl.ds(which, 1), :]
                gb[layer, which, kind] = jnp.transpose(jnp.broadcast_to(line, (CH, CH)))


def project(layer, pair, i, inside, wt, gb, gating, fact):
    gain, bias = gb[layer, 0, 0], gb[layer, 0, 1]
    zn = jnp.concatenate([norm(z, gain, bias) for z in pair], axis=1)
    p = jnp.dot(wt[layer], zn, preferred_element_type=F32)
    for e in range(2):
        q = p[:, e * CH : (e + 1) * CH]
        left = jnp.where(inside, sigmoid(q[:CH]) * q[CH : 2 * CH], 0.0)
        right = jnp.where(inside, sigmoid(q[2 * CH : 3 * CH]) * q[3 * CH : 4 * CH], 0.0)
        fact[0, pl.ds(i + e, CH, stride=HALF), :] = left
        fact[1, pl.ds(i + e, CH, stride=HALF), :] = right
        gating[e] = sigmoid(q[4 * CH :])


def pack(fact, send):
    def step(t, carry):
        for f in range(2):
            block = fact[f, pl.ds(pl.multiple_of(t * 256, 256), 256), :]
            send[pl.ds(t * 16, 16), f] = block.reshape(16, HALF, CH).astype(BF16)
        return carry

    lax.fori_loop(0, 8, step, 0)


def first_half(half, z_ref, inside, wt, gb, zt, gating, fact, send):
    def step(t, carry):
        i = 2 * t
        row = half * HALF + i
        pair = [flip(z_ref[row + e]) for e in range(2)]
        for e in range(2):
            zt[row + e] = pair[e].astype(BF16)
        project(0, pair, i, inside, wt, gb, gating.at[pl.ds(row, 2)], fact)
        return carry

    lax.fori_loop(0, HALF // 2, step, 0)
    pack(fact, send)


def updated(layer, row, i, inside, wo, gb, zt, gating, sums):
    gain, bias = gb[layer, 1, 0], gb[layer, 1, 1]
    normed = jnp.concatenate(
        [norm(sums[pl.ds(i + e, CH, stride=HALF), :], gain, bias) for e in range(2)], axis=1
    )
    u = jnp.dot(wo[layer], normed, preferred_element_type=F32)
    return [
        jnp.where(
            inside, zt[row + e].astype(F32) + gating[row + e] * u[:, e * CH : (e + 1) * CH], 0.0
        ).astype(BF16)
        for e in range(2)
    ]


def unpack(got, sums):
    def step(t, carry):
        block = got[pl.ds(t * 16, 16)].astype(F32)
        sums[pl.ds(pl.multiple_of(t * 256, 256), 256), :] = block.reshape(256, CH)
        return carry

    lax.fori_loop(0, 8, step, 0)


def middle_half(half, got, inside, wt, wo, gb, zt, gating, sums, fact, send):
    unpack(got, sums)

    def step(t, carry):
        i = 2 * t
        row = half * HALF + i
        pair = updated(0, row, i, inside, wo, gb, zt, gating, sums)
        for e in range(2):
            zt[row + e] = pair[e]
        project(
            1, [z.astype(F32) for z in pair], i, inside, wt, gb, gating.at[pl.ds(row, 2)], fact
        )
        return carry

    lax.fori_loop(0, HALF // 2, step, 0)
    pack(fact, send)


def last_half(half, got, inside, wo, gb, zt, gating, sums, o_ref):
    unpack(got, sums)

    def step(t, carry):
        i = 2 * t
        row = half * HALF + i
        pair = updated(1, row, i, inside, wo, gb, zt, gating, sums)
        for e in range(2):
            o_ref[row + e] = flip(pair[e]).astype(BF16)
        return carry

    lax.fori_loop(0, HALF // 2, step, 0)


def triangle(layer, begin_ref, extent_ref, recv, block_sums):
    dims = (((1,), (1,)), ((), ())) if layer == 0 else (((0,), (0,)), ((), ()))

    def step(b, carry):
        begin = begin_ref[b]
        ours = lax.broadcasted_iota(jnp.int32, (SPAN, HALF, CH), 0) < extent_ref[b]

        def window(f):
            tall = []
            for half in range(2):
                wide = [
                    jnp.where(ours, recv[pl.ds(begin, SPAN), h, half, f], jnp.zeros((), BF16)).reshape(CH, CH)
                    for h in range(2)
                ]
                tall.append(jnp.concatenate(wide, axis=1))
            return jnp.concatenate(tall, axis=0)

        s = lax.dot_general(window(0), window(1), dims, preferred_element_type=F32).astype(BF16)
        for hi in range(2):
            for hj in range(2):
                block_sums[b, hj, hi] = s[hi * CH : (hi + 1) * CH, hj * CH : (hj + 1) * CH].reshape(
                    SPAN, HALF, CH
                )
        return carry

    lax.fori_loop(0, COMPLEXES, step, 0)


def spread(member_ref, place_ref, block_sums, send, half):
    def step(r, carry):
        b, q = member_ref[r], place_ref[r]
        for hj in range(2):
            send[2 * r + hj] = block_sums[b, hj, half, q]
        return carry

    lax.fori_loop(0, DEV_ROWS, step, 0)


def inside_mask(extent):
    return lax.broadcasted_iota(jnp.int32, (1, CH), 1) < extent * HALF


def k_first(own_ref, z_ref, gain_ref, bias_ref, proj_ref, gate_ref, outw_ref, zt, gating, send, wt, wo, gb, fact):
    prepare(gain_ref, bias_ref, proj_ref, gate_ref, outw_ref, wt, wo, gb)
    inside = inside_mask(own_ref[0])
    for half in range(2):
        first_half(half, z_ref, inside, wt, gb, zt, gating, fact, send.at[half])


def k_triangle(layer, begin_ref, extent_ref, member_ref, place_ref, got, send, recv, block_sums):
    recv[pl.ds(DEV_ROWS, SPAN)] = jnp.zeros((SPAN,) + recv.shape[1:], BF16)

    def move(r, carry):
        for half in range(2):
            for h in range(2):
                recv[r, h, half] = got[half, 2 * r + h]
        return carry

    lax.fori_loop(0, DEV_ROWS, move, 0)
    triangle(layer, begin_ref, extent_ref, recv, block_sums)
    for half in range(2):
        spread(member_ref, place_ref, block_sums, send.at[half], half)


def k_middle(own_ref, got, zt_in, gating_in, wt, wo, gb, zt, gating, send, sums, fact):
    inside = inside_mask(own_ref[0])
    zt[...] = zt_in[...]
    gating[...] = gating_in[...]
    for half in range(2):
        middle_half(half, got.at[half], inside, wt, wo, gb, zt, gating, sums, fact, send.at[half])


def k_last(own_ref, got, zt, gating, wo, gb, o_ref, sums):
    inside = inside_mask(own_ref[0])
    for half in range(2):
        last_half(half, got.at[half], inside, wo, gb, zt, gating, sums, o_ref)


def body(pair_rep, token_counts, first_device, norm_gain, norm_bias, proj_weight, gate_weight, out_weight):
    row = lax.axis_index("row")
    extents = token_counts // ROWS
    rows = jnp.arange(DEV_ROWS, dtype=jnp.int32)
    member = jnp.sum((first_device[None, :] <= rows[:, None]).astype(jnp.int32), 1) - 1
    place = rows - first_device[member]
    own = extents[member[row]].reshape(1)
    smem = pl.BlockSpec(memory_space=pltpu.SMEM)
    vmem = pl.BlockSpec(memory_space=pltpu.VMEM)
    params = pltpu.CompilerParams(vmem_limit_bytes=48 * 2**20)
    S = jax.ShapeDtypeStruct
    zt_s, gating_s = S((ROWS, CH, CH), BF16), S((ROWS, CH, CH), F32)
    send_s = S((2, DEVS, 2, HALF, CH), BF16)
    back_s = S((2, DEVS, HALF, CH), BF16)
    wt_s, wo_s, gb_s = S((2, 5 * CH, CH), BF16), S((2, CH, CH), BF16), S((2, 2, 2, CH, CH), F32)
    fact_s = pltpu.VMEM((2, CH * HALF, CH), F32)
    sums_s = pltpu.VMEM((CH * HALF, CH), F32)

    def a2a(x):
        return lax.all_to_all(x, ("row", "col"), 1, 1, tiled=True)

    def tri(layer, got):
        return pl.pallas_call(
            functools.partial(k_triangle, layer),
            out_shape=back_s,
            in_specs=[smem] * 4 + [vmem],
            out_specs=vmem,
            scratch_shapes=[
                pltpu.VMEM((DEV_ROWS + SPAN, 2, 2, 2, HALF, CH), BF16),
                pltpu.VMEM((COMPLEXES, 2, 2, SPAN, HALF, CH), BF16),
            ],
            compiler_params=params,
        )(first_device, extents, member, place, got)

    zt, gating, send, wt, wo, gb = pl.pallas_call(
        k_first,
        out_shape=(zt_s, gating_s, send_s, wt_s, wo_s, gb_s),
        in_specs=[smem] + [vmem] * 6,
        out_specs=[vmem] * 6,
        scratch_shapes=[fact_s],
        compiler_params=params,
    )(own, pair_rep, norm_gain, norm_bias, proj_weight, gate_weight, out_weight)
    back = a2a(tri(0, a2a(send)))
    zt, gating, send = pl.pallas_call(
        k_middle,
        out_shape=(zt_s, gating_s, send_s),
        in_specs=[smem] + [vmem] * 6,
        out_specs=[vmem] * 3,
        scratch_shapes=[sums_s, fact_s],
        compiler_params=params,
    )(own, back, zt, gating, wt, wo, gb)
    back = a2a(tri(1, a2a(send)))
    return pl.pallas_call(
        k_last,
        out_shape=S((ROWS, CH, CH), BF16),
        in_specs=[smem] + [vmem] * 5,
        out_specs=vmem,
        scratch_shapes=[sums_s],
        compiler_params=params,
    )(own, back, zt, gating, wo, gb)


def solution(mesh):
    return jax.shard_map(
        body,
        mesh=mesh,
        in_specs=(P("row", "col", None), P(), P(), P(), P(), P(), P(), P()),
        out_specs=P("row", "col", None),
        check_vma=False,
    )
```

```python
import functools

import jax
import jax.numpy as jnp
from jax import lax
from jax.experimental import pallas as pl
from jax.experimental.pallas import tpu as pltpu
from jax.sharding import PartitionSpec as P

EPS = 1e-05
CH = 128
ROWS = 32
HALF = 16
SPAN = 8
COMPLEXES = 16
DEV_ROWS = 64
DEVS = 128
F32 = jnp.float32
BF16 = jnp.bfloat16
MESH = pl.DeviceIdType.MESH


def sigmoid(x):
    return 0.5 * jnp.tanh(0.5 * x) + 0.5


def flip(x):
    eye = (
        lax.broadcasted_iota(jnp.int32, (CH, CH), 0) == lax.broadcasted_iota(jnp.int32, (CH, CH), 1)
    ).astype(F32).astype(BF16)
    return lax.dot_general(eye, x, (((1,), (1,)), ((), ())), preferred_element_type=F32)


def norm(x, gain, bias):
    average = jnp.sum(x, axis=0, keepdims=True) * (1.0 / CH)
    centred = x - average
    variance = jnp.sum(centred * centred, axis=0, keepdims=True) * (1.0 / CH)
    return (centred * lax.rsqrt(variance + EPS) * gain + bias).astype(BF16)


def prepare(gain_ref, bias_ref, proj_ref, gate_ref, out_ref, wt, wo, gb):
    for layer in range(2):
        for blk in range(4):
            part = slice(blk * CH, (blk + 1) * CH)
            wt[layer, part] = flip(proj_ref[layer, :, part]).astype(BF16)
        wt[layer, 4 * CH :] = flip(gate_ref[layer]).astype(BF16)
        wo[layer] = flip(out_ref[layer]).astype(BF16)
        for which in range(2):
            for kind, ref in enumerate((gain_ref, bias_ref)):
                line = ref[layer, pl.ds(which, 1), :]
                gb[layer, which, kind] = jnp.transpose(jnp.broadcast_to(line, (CH, CH)))


def project(layer, pair, i, inside, wt, gb, gating, fact):
    gain, bias = gb[layer, 0, 0], gb[layer, 0, 1]
    zn = jnp.concatenate([norm(z, gain, bias) for z in pair], axis=1)
    p = jnp.dot(wt[layer], zn, preferred_element_type=F32)
    for e in range(2):
        q = p[:, e * CH : (e + 1) * CH]
        left = jnp.where(inside, sigmoid(q[:CH]) * q[CH : 2 * CH], 0.0)
        right = jnp.where(inside, sigmoid(q[2 * CH : 3 * CH]) * q[3 * CH : 4 * CH], 0.0)
        fact[0, pl.ds(i + e, CH, stride=HALF), :] = left
        fact[1, pl.ds(i + e, CH, stride=HALF), :] = right
        gating[e] = sigmoid(q[4 * CH :])


def pack(fact, send):
    def step(t, carry):
        for f in range(2):
            block = fact[f, pl.ds(pl.multiple_of(t * 256, 256), 256), :]
            send[pl.ds(t * 16, 16), f] = block.reshape(16, HALF, CH).astype(BF16)
        return carry

    lax.fori_loop(0, 8, step, 0)


def first_half(half, z_ref, inside, wt, gb, zt, gating, fact, send):
    def step(t, carry):
        i = 2 * t
        row = half * HALF + i
        pair = [flip(z_ref[row + e]) for e in range(2)]
        for e in range(2):
            zt[row + e] = pair[e].astype(BF16)
        project(0, pair, i, inside, wt, gb, gating.at[pl.ds(row, 2)], fact)
        return carry

    lax.fori_loop(0, HALF // 2, step, 0)
    pack(fact, send)


def updated(layer, row, i, inside, wo, gb, zt, gating, sums):
    gain, bias = gb[layer, 1, 0], gb[layer, 1, 1]
    normed = jnp.concatenate(
        [norm(sums[pl.ds(i + e, CH, stride=HALF), :], gain, bias) for e in range(2)], axis=1
    )
    u = jnp.dot(wo[layer], normed, preferred_element_type=F32)
    return [
        jnp.where(
            inside, zt[row + e].astype(F32) + gating[row + e] * u[:, e * CH : (e + 1) * CH], 0.0
        ).astype(BF16)
        for e in range(2)
    ]


def unpack(got, sums):
    def step(t, carry):
        block = got[pl.ds(t * 16, 16)].astype(F32)
        sums[pl.ds(pl.multiple_of(t * 256, 256), 256), :] = block.reshape(256, CH)
        return carry

    lax.fori_loop(0, 8, step, 0)


def middle_half(half, got, inside, wt, wo, gb, zt, gating, sums, fact, send):
    unpack(got, sums)

    def step(t, carry):
        i = 2 * t
        row = half * HALF + i
        pair = updated(0, row, i, inside, wo, gb, zt, gating, sums)
        for e in range(2):
            zt[row + e] = pair[e]
        project(
            1, [z.astype(F32) for z in pair], i, inside, wt, gb, gating.at[pl.ds(row, 2)], fact
        )
        return carry

    lax.fori_loop(0, HALF // 2, step, 0)
    pack(fact, send)


def last_half(half, got, inside, wo, gb, zt, gating, sums, o_ref):
    unpack(got, sums)

    def step(t, carry):
        i = 2 * t
        row = half * HALF + i
        pair = updated(1, row, i, inside, wo, gb, zt, gating, sums)
        for e in range(2):
            o_ref[row + e] = flip(pair[e]).astype(BF16)
        return carry

    lax.fori_loop(0, HALF // 2, step, 0)


def triangle(layer, begin_ref, count_ref, recv, block_sums):
    dims = (((1,), (1,)), ((), ())) if layer == 0 else (((0,), (0,)), ((), ()))

    def step(b, carry):
        begin = jnp.clip(begin_ref[b], 0, DEV_ROWS - 1)
        ours = lax.broadcasted_iota(jnp.int32, (SPAN, HALF, CH), 0) * ROWS < count_ref[b]

        parts = [
            recv[half][pl.ds(2 * begin, 2 * SPAN)].reshape(SPAN, 2, 2, HALF, CH) for half in range(2)
        ]

        def window(f):
            tall = []
            for half in range(2):
                wide = [
                    jnp.where(ours, parts[half][:, h, f], jnp.zeros((), BF16)).reshape(CH, CH)
                    for h in range(2)
                ]
                tall.append(jnp.concatenate(wide, axis=1))
            return jnp.concatenate(tall, axis=0)

        s = lax.dot_general(window(0), window(1), dims, preferred_element_type=F32).astype(BF16)
        for hi in range(2):
            for hj in range(2):
                block_sums[b, hj, hi] = s[hi * CH : (hi + 1) * CH, hj * CH : (hj + 1) * CH].reshape(
                    SPAN, HALF, CH
                )
        return carry

    lax.fori_loop(0, COMPLEXES, step, 0)


def spread(begin_ref, block_sums, send):
    def step(r, b):
        later = jnp.minimum(b + 1, COMPLEXES - 1)
        b = jnp.where(begin_ref[later] <= r, later, b)
        q = jnp.clip(r - begin_ref[b], 0, SPAN - 1)
        for half in range(2):
            for hj in range(2):
                send[half][2 * r + hj] = block_sums[b, hj, half, q]
        return b

    lax.fori_loop(0, DEV_ROWS, step, jnp.int32(0))


def inside_mask(row, begin_ref, count_ref):
    count = count_ref[0]
    for b in range(1, COMPLEXES):
        count = jnp.where(begin_ref[b] <= row, count_ref[b], count)
    return lax.broadcasted_iota(jnp.int32, (1, CH), 1) * 2 < count


def kernel(
    count_ref, begin_ref, z_hbm, gain_hbm, bias_hbm, proj_hbm, gate_hbm, outw_hbm,
    o_ref,
    z_ref, gain_ref, bias_ref, proj_ref, gate_ref, outw_ref,
    wt, wo, gb, zt, gating, fact, sums, block_sums, load_sem, send_sem, recv_sem, *exchanged,
):
    send, recv, back, got = [
        [exchanged[k : k + 2], exchanged[k + 2 : k + 4]] for k in range(0, 16, 4)
    ]
    row, col = lax.axis_index("row"), lax.axis_index("col")
    me = row * 2 + col
    y, x, z = row // 16, (row // 4) % 4, row % 4

    def peer(s):
        to = ((y + s // 32) % 4) * 16 + ((x + (s // 8) % 4) % 4) * 4 + (z + (s // 2) % 4) % 4
        return to, (col + s) % 2

    loads = [
        pltpu.make_async_copy(src, dst, load_sem.at[k])
        for k, (src, dst) in enumerate(
            (
                (proj_hbm, proj_ref),
                (gate_hbm, gate_ref),
                (outw_hbm, outw_ref),
                (gain_hbm, gain_ref),
                (bias_hbm, bias_ref),
                (z_hbm, z_ref),
            )
        )
    ]
    for load in loads:
        load.start()

    for ref in recv[0] + recv[1]:
        ref[pl.ds(DEVS, 2 * SPAN)] = jnp.zeros((2 * SPAN,) + ref.shape[1:], BF16)

    barrier = pltpu.get_barrier_semaphore()

    def greet(s, carry):
        pl.semaphore_signal(barrier, inc=1, device_id=peer(s), device_id_type=MESH)
        return carry

    lax.fori_loop(1, DEVS, greet, 0)

    inside = inside_mask(row, begin_ref, count_ref)
    for load in loads:
        load.wait()
    prepare(gain_ref, bias_ref, proj_ref, gate_ref, outw_ref, wt, wo, gb)

    def deliver(src, dst, k):
        def step(s, carry):
            to, core = peer((s * 37) % DEVS)
            pltpu.make_async_remote_copy(
                src_ref=src.at[to * 2 + core],
                dst_ref=dst.at[me],
                send_sem=send_sem.at[k],
                recv_sem=recv_sem.at[k],
                device_id=(to, core),
                device_id_type=MESH,
            ).start()
            return carry

        lax.fori_loop(1, DEVS, step, 0)

    def others(src, dst, k):
        return pltpu.make_async_remote_copy(
            src_ref=src.at[pl.ds(0, DEVS - 1)],
            dst_ref=dst.at[pl.ds(0, DEVS - 1)],
            send_sem=send_sem.at[k],
            recv_sem=recv_sem.at[k],
            device_id=(row, 1 - col),
            device_id_type=MESH,
        )

    def arrived(src, dst, k):
        others(src, dst, k).wait_recv()
        dst[me] = src[me]

    def forward(layer, half):
        return send[layer][half], recv[layer][half], 4 * layer + half

    def backward(layer, half):
        return back[layer][half], got[layer][half], 4 * layer + 2 + half

    def product(layer):
        for half in range(2):
            arrived(*forward(layer, half))
        triangle(layer, begin_ref, count_ref, recv[layer], block_sums)
        spread(begin_ref, block_sums, back[layer])
        for half in range(2):
            deliver(*backward(layer, half))

    for half in range(2):
        first_half(half, z_ref, inside, wt, gb, zt, gating, fact, send[0][half])
        if half == 0:
            pl.semaphore_wait(barrier, DEVS - 1)
        deliver(*forward(0, half))
    product(0)
    for half in range(2):
        arrived(*backward(0, half))
        middle_half(
            half, got[0][half], inside, wt, wo, gb, zt, gating, sums, fact, send[1][half]
        )
        deliver(*forward(1, half))
    product(1)
    for half in range(2):
        arrived(*backward(1, half))
        last_half(half, got[1][half], inside, wo, gb, zt, gating, sums, o_ref)
    for layer in range(2):
        for half in range(2):
            others(*forward(layer, half)).wait_send()
            others(*backward(layer, half)).wait_send()


def body(pair_rep, token_counts, first_device, norm_gain, norm_bias, proj_weight, gate_weight, out_weight):
    smem = pl.BlockSpec(memory_space=pltpu.SMEM)
    anywhere = pl.BlockSpec(memory_space=pl.ANY)
    loaded = (pair_rep, norm_gain, norm_bias, proj_weight, gate_weight, out_weight)
    return pl.pallas_call(
        kernel,
        out_shape=jax.ShapeDtypeStruct(pair_rep.shape, BF16),
        in_specs=[smem] * 2 + [anywhere] * 6,
        out_specs=pl.BlockSpec(memory_space=pltpu.VMEM),
        scratch_shapes=[pltpu.VMEM(a.shape, a.dtype) for a in loaded]
        + [
            pltpu.VMEM((2, 5 * CH, CH), BF16),
            pltpu.VMEM((2, CH, CH), BF16),
            pltpu.VMEM((2, 2, 2, CH, CH), F32),
            pltpu.VMEM((ROWS, CH, CH), BF16),
            pltpu.VMEM((ROWS, CH, CH), F32),
            pltpu.VMEM((2, CH * HALF, CH), F32),
            pltpu.VMEM((CH * HALF, CH), F32),
            pltpu.VMEM((COMPLEXES, 2, 2, SPAN, HALF, CH), BF16),
            pltpu.SemaphoreType.DMA((6,)),
            pltpu.SemaphoreType.DMA((8,)),
            pltpu.SemaphoreType.DMA((8,)),
        ]
        + [pltpu.VMEM((DEVS, 2, HALF, CH), BF16)] * 4
        + [pltpu.VMEM((DEVS + 2 * SPAN, 2, HALF, CH), BF16)] * 4
        + [pltpu.VMEM((DEVS, HALF, CH), BF16)] * 8,
        compiler_params=pltpu.CompilerParams(
            collective_id=0, has_side_effects=True, vmem_limit_bytes=56 * 2**20
        ),
        cost_estimate=pl.CostEstimate(
            flops=3 * 10**9, bytes_accessed=16 * 2**20, transcendentals=6 * 2**20
        ),
    )(token_counts, first_device, *loaded)


def solution(mesh):
    return jax.shard_map(
        body,
        mesh=mesh,
        in_specs=(P("row", "col", None), P(), P(), P(), P(), P(), P(), P()),
        out_specs=P("row", "col", None),
        check_vma=False,
    )
```

```python
import functools

import jax
import jax.numpy as jnp
from jax import lax
from jax.experimental import pallas as pl
from jax.experimental.pallas import tpu as pltpu
from jax.sharding import PartitionSpec as P

EPS = 1e-05
CH = 128
ROWS = 32
HALF = 16
SPAN = 8
COMPLEXES = 16
DEV_ROWS = 64
DEVS = 128
F32 = jnp.float32
BF16 = jnp.bfloat16
MESH = pl.DeviceIdType.MESH


def sigmoid(x):
    return 0.5 * jnp.tanh(0.5 * x) + 0.5


def flip(x):
    eye = (
        lax.broadcasted_iota(jnp.int32, (CH, CH), 0) == lax.broadcasted_iota(jnp.int32, (CH, CH), 1)
    ).astype(F32).astype(BF16)
    return lax.dot_general(eye, x, (((1,), (1,)), ((), ())), preferred_element_type=F32)


def norm(x, gain, bias):
    average = jnp.sum(x, axis=0, keepdims=True) * (1.0 / CH)
    centred = x - average
    variance = jnp.sum(centred * centred, axis=0, keepdims=True) * (1.0 / CH)
    return (centred * lax.rsqrt(variance + EPS) * gain + bias).astype(BF16)


def prepare(gain_ref, bias_ref, proj_ref, gate_ref, out_ref, wt, wo, gb):
    for layer in range(2):
        for blk in range(4):
            part = slice(blk * CH, (blk + 1) * CH)
            wt[layer, part] = flip(proj_ref[layer, :, part]).astype(BF16)
        wt[layer, 4 * CH :] = flip(gate_ref[layer]).astype(BF16)
        wo[layer] = flip(out_ref[layer]).astype(BF16)
        for which in range(2):
            for kind, ref in enumerate((gain_ref, bias_ref)):
                line = ref[layer, pl.ds(which, 1), :]
                gb[layer, which, kind] = jnp.transpose(jnp.broadcast_to(line, (CH, CH)))


def project(layer, pair, i, inside, wt, gb, gating, fact):
    gain, bias = gb[layer, 0, 0], gb[layer, 0, 1]
    zn = jnp.concatenate([norm(z, gain, bias) for z in pair], axis=1)
    p = jnp.dot(wt[layer], zn, preferred_element_type=F32)
    for e in range(2):
        q = p[:, e * CH : (e + 1) * CH]
        left = jnp.where(inside, sigmoid(q[:CH]) * q[CH : 2 * CH], 0.0)
        right = jnp.where(inside, sigmoid(q[2 * CH : 3 * CH]) * q[3 * CH : 4 * CH], 0.0)
        fact[0, pl.ds(i + e, CH, stride=HALF), :] = left
        fact[1, pl.ds(i + e, CH, stride=HALF), :] = right
        gating[e] = sigmoid(q[4 * CH :])


def pack(fact, send):
    def step(t, carry):
        for f in range(2):
            block = fact[f, pl.ds(pl.multiple_of(t * 256, 256), 256), :]
            send[f][pl.ds(t * 16, 16)] = block.reshape(16, HALF, CH).astype(BF16)
        return carry

    lax.fori_loop(0, 8, step, 0)


def first_half(half, z_ref, inside, wt, gb, zt, gating, fact, send):
    def step(t, carry):
        i = 2 * t
        row = half * HALF + i
        pair = [flip(z_ref[row + e]) for e in range(2)]
        for e in range(2):
            zt[row + e] = pair[e].astype(BF16)
        project(0, pair, i, inside, wt, gb, gating.at[pl.ds(row, 2)], fact)
        return carry

    lax.fori_loop(0, HALF // 2, step, 0)
    pack(fact, send)


def updated(layer, row, i, inside, wo, gb, zt, gating, sums):
    gain, bias = gb[layer, 1, 0], gb[layer, 1, 1]
    normed = jnp.concatenate(
        [norm(sums[pl.ds(i + e, CH, stride=HALF), :], gain, bias) for e in range(2)], axis=1
    )
    u = jnp.dot(wo[layer], normed, preferred_element_type=F32)
    return [
        jnp.where(
            inside, zt[row + e].astype(F32) + gating[row + e] * u[:, e * CH : (e + 1) * CH], 0.0
        ).astype(BF16)
        for e in range(2)
    ]


def unpack(got, sums):
    def step(t, carry):
        block = got[pl.ds(t * 16, 16)].astype(F32)
        sums[pl.ds(pl.multiple_of(t * 256, 256), 256), :] = block.reshape(256, CH)
        return carry

    lax.fori_loop(0, 8, step, 0)


def middle_half(half, got, inside, wt, wo, gb, zt, gating, sums, fact, send):
    unpack(got, sums)

    def step(t, carry):
        i = 2 * t
        row = half * HALF + i
        pair = updated(0, row, i, inside, wo, gb, zt, gating, sums)
        for e in range(2):
            zt[row + e] = pair[e]
        project(
            1, [z.astype(F32) for z in pair], i, inside, wt, gb, gating.at[pl.ds(row, 2)], fact
        )
        return carry

    lax.fori_loop(0, HALF // 2, step, 0)
    pack(fact, send)


def last_half(half, got, inside, wo, gb, zt, gating, sums, o_ref):
    unpack(got, sums)

    def step(t, carry):
        i = 2 * t
        row = half * HALF + i
        pair = updated(1, row, i, inside, wo, gb, zt, gating, sums)
        for e in range(2):
            o_ref[row + e] = flip(pair[e]).astype(BF16)
        return carry

    lax.fori_loop(0, HALF // 2, step, 0)


def window(ref, begin, ours, cores=(0, 1)):
    part = ref[pl.ds(2 * begin, 2 * SPAN)].reshape(SPAN, 2, HALF, CH)
    return jnp.concatenate(
        [jnp.where(ours, part[:, h], jnp.zeros((), BF16)).reshape(CH, CH) for h in cores], axis=1
    )


def per_complex(begin_ref, count_ref, work):
    def step(b, carry):
        begin = jnp.clip(begin_ref[b], 0, DEV_ROWS - 1)
        ours = lax.broadcasted_iota(jnp.int32, (SPAN, HALF, CH), 0) * ROWS < count_ref[b]
        work(b, begin, ours)
        return carry

    lax.fori_loop(0, COMPLEXES, step, 0)


def keep(block_sums, b, sums):
    for core in range(2):
        block_sums[b, core] = sums[:, core * CH : (core + 1) * CH].astype(BF16).reshape(SPAN, HALF, CH)


def outgoing(begin_ref, count_ref, left, right, block_sums):
    def work(b, begin, ours):
        them = jnp.concatenate([window(ref, begin, ours) for ref in right], axis=0)
        sums = lax.dot_general(
            window(left, begin, ours), them, (((1,), (1,)), ((), ())), preferred_element_type=F32
        )
        keep(block_sums, b, sums)

    per_complex(begin_ref, count_ref, work)


def incoming_start(begin_ref, count_ref, left, right, partial):
    def work(b, begin, ours):
        partial[b] = lax.dot_general(
            window(left, begin, ours),
            window(right, begin, ours),
            (((0,), (0,)), ((), ())),
            preferred_element_type=F32,
        )

    per_complex(begin_ref, count_ref, work)


def incoming_end(begin_ref, count_ref, left, right, partial, core, block_sums):
    def work(b, begin, ours):
        sums = partial[b, core * CH : (core + 1) * CH] + lax.dot_general(
            window(left, begin, ours, (core,)),
            window(right, begin, ours),
            (((0,), (0,)), ((), ())),
            preferred_element_type=F32,
        )
        keep(block_sums, b, sums)

    per_complex(begin_ref, count_ref, work)


def spread(begin_ref, block_sums, send):
    def step(r, b):
        later = jnp.minimum(b + 1, COMPLEXES - 1)
        b = jnp.where(begin_ref[later] <= r, later, b)
        q = jnp.clip(r - begin_ref[b], 0, SPAN - 1)
        for core in range(2):
            send[2 * r + core] = block_sums[b, core, q]
        return b

    lax.fori_loop(0, DEV_ROWS, step, jnp.int32(0))


def inside_mask(row, begin_ref, count_ref):
    count = count_ref[0]
    for b in range(1, COMPLEXES):
        count = jnp.where(begin_ref[b] <= row, count_ref[b], count)
    return lax.broadcasted_iota(jnp.int32, (1, CH), 1) * 2 < count


def kernel(
    count_ref, begin_ref, z_hbm, gain_hbm, bias_hbm, proj_hbm, gate_hbm, outw_hbm,
    o_ref,
    z_ref, gain_ref, bias_ref, proj_ref, gate_ref, outw_ref,
    wt, wo, gb, zt, gating, fact, sums, block_sums, partial, load_sem, send_sem, recv_sem, *exchanged,
):
    send, recv, back, got = exchanged[:5], exchanged[5:10], exchanged[10:14], exchanged[14:18]
    row, col = lax.axis_index("row"), lax.axis_index("col")
    me = row * 2 + col
    y, x, z = row >> 4, (row >> 2) & 3, row & 3
    planes = [((y + dy) & 3) * 16 for dy in range(4)]
    cores = (col, 1 - col)

    def peers(work):
        def group(t, first):
            for dy in range(4):
                to = planes[dy] + ((x + (t >> 2) + dy) & 3) * 4 + ((z + t + dy) & 3)
                for core in cores[first:] if dy == 0 else cores:
                    work(to, core)

        def step(t, carry):
            group(t, 0)
            return carry

        group(0, 1)
        lax.fori_loop(1, 16, step, 0)

    loads = [
        pltpu.make_async_copy(src, dst, load_sem.at[k])
        for k, (src, dst) in enumerate(
            (
                (proj_hbm, proj_ref),
                (gate_hbm, gate_ref),
                (outw_hbm, outw_ref),
                (gain_hbm, gain_ref),
                (bias_hbm, bias_ref),
                (z_hbm, z_ref),
            )
        )
    ]
    for load in loads:
        load.start()

    for ref in recv:
        ref[pl.ds(DEVS, 2 * SPAN)] = jnp.zeros((2 * SPAN,) + ref.shape[1:], BF16)

    barrier = pltpu.get_barrier_semaphore()

    peers(
        lambda to, core: pl.semaphore_signal(
            barrier, inc=1, device_id=(to, core), device_id_type=MESH
        )
    )

    inside = inside_mask(row, begin_ref, count_ref)
    for load in loads:
        load.wait()
    prepare(gain_ref, bias_ref, proj_ref, gate_ref, outw_ref, wt, wo, gb)

    def deliver(src, dst, k):
        def copy(to, core):
            pltpu.make_async_remote_copy(
                src_ref=src.at[to * 2 + core],
                dst_ref=dst.at[me],
                send_sem=send_sem.at[k],
                recv_sem=recv_sem.at[k],
                device_id=(to, core),
                device_id_type=MESH,
            ).start()

        peers(copy)

    def others(src, dst, k):
        return pltpu.make_async_remote_copy(
            src_ref=src.at[pl.ds(0, DEVS - 1)],
            dst_ref=dst.at[pl.ds(0, DEVS - 1)],
            send_sem=send_sem.at[k],
            recv_sem=recv_sem.at[k],
            device_id=(row, 1 - col),
            device_id_type=MESH,
        )

    def arrived(src, dst, k):
        others(src, dst, k).wait_recv()
        dst[me] = src[me]

    def forward(k):
        return send[k], recv[k], k

    def backward(k):
        return back[k], got[k], 5 + k

    def factors(refs, k):
        return [refs[k].at[:, f] for f in range(2)]

    def to_back(k):
        spread(begin_ref, block_sums, back[k])
        deliver(*backward(k))

    first_half(0, z_ref, inside, wt, gb, zt, gating, fact, factors(send, 0))
    pl.semaphore_wait(barrier, DEVS - 1)
    deliver(*forward(0))
    first_half(1, z_ref, inside, wt, gb, zt, gating, fact, (send[2], send[1]))
    deliver(*forward(1))
    deliver(*forward(2))

    arrived(*forward(0))
    arrived(*forward(1))
    left, right = factors(recv, 0)
    outgoing(begin_ref, count_ref, left, (right, recv[1]), block_sums)
    to_back(0)
    arrived(*forward(2))
    outgoing(begin_ref, count_ref, recv[2], (right, recv[1]), block_sums)
    to_back(1)

    for half in range(2):
        arrived(*backward(half))
        middle_half(
            half, got[half], inside, wt, wo, gb, zt, gating, sums, fact, factors(send, 3 + half)
        )
        deliver(*forward(3 + half))

    arrived(*forward(3))
    incoming_start(begin_ref, count_ref, *factors(recv, 3), partial)
    arrived(*forward(4))
    for core in range(2):
        incoming_end(begin_ref, count_ref, *factors(recv, 4), partial, core, block_sums)
        to_back(2 + core)

    for half in range(2):
        arrived(*backward(2 + half))
        last_half(half, got[2 + half], inside, wo, gb, zt, gating, sums, o_ref)
    for k in range(5):
        others(*forward(k)).wait_send()
    for k in range(4):
        others(*backward(k)).wait_send()


def body(pair_rep, token_counts, first_device, norm_gain, norm_bias, proj_weight, gate_weight, out_weight):
    smem = pl.BlockSpec(memory_space=pltpu.SMEM)
    anywhere = pl.BlockSpec(memory_space=pl.ANY)
    both, one = (2, HALF, CH), (HALF, CH)
    forms = (both, one, one, both, both)
    loaded = (pair_rep, norm_gain, norm_bias, proj_weight, gate_weight, out_weight)
    return pl.pallas_call(
        kernel,
        out_shape=jax.ShapeDtypeStruct(pair_rep.shape, BF16),
        in_specs=[smem] * 2 + [anywhere] * 6,
        out_specs=pl.BlockSpec(memory_space=pltpu.VMEM),
        scratch_shapes=[pltpu.VMEM(a.shape, a.dtype) for a in loaded]
        + [
            pltpu.VMEM((2, 5 * CH, CH), BF16),
            pltpu.VMEM((2, CH, CH), BF16),
            pltpu.VMEM((2, 2, 2, CH, CH), F32),
            pltpu.VMEM((ROWS, CH, CH), BF16),
            pltpu.VMEM((ROWS, CH, CH), F32),
            pltpu.VMEM((2, CH * HALF, CH), F32),
            pltpu.VMEM((CH * HALF, CH), F32),
            pltpu.VMEM((COMPLEXES, 2, SPAN, HALF, CH), BF16),
            pltpu.VMEM((COMPLEXES, 2 * CH, 2 * CH), F32),
            pltpu.SemaphoreType.DMA((6,)),
            pltpu.SemaphoreType.DMA((9,)),
            pltpu.SemaphoreType.DMA((9,)),
        ]
        + [pltpu.VMEM((DEVS,) + form, BF16) for form in forms]
        + [pltpu.VMEM((DEVS + 2 * SPAN,) + form, BF16) for form in forms]
        + [pltpu.VMEM((DEVS, HALF, CH), BF16)] * 8,
        compiler_params=pltpu.CompilerParams(
            collective_id=0, has_side_effects=True, vmem_limit_bytes=56 * 2**20
        ),
        cost_estimate=pl.CostEstimate(
            flops=3 * 10**9, bytes_accessed=16 * 2**20, transcendentals=6 * 2**20
        ),
    )(token_counts, first_device, *loaded)


def solution(mesh):
    return jax.shard_map(
        body,
        mesh=mesh,
        in_specs=(P("row", "col", None), P(), P(), P(), P(), P(), P(), P()),
        out_specs=P("row", "col", None),
        check_vma=False,
    )
```

```python
import functools

import jax
import jax.numpy as jnp
from jax import lax
from jax.experimental import pallas as pl
from jax.experimental.pallas import tpu as pltpu
from jax.sharding import PartitionSpec as P

EPS = 1e-05
CH = 128
ROWS = 32
HALF = 16
SPAN = 8
COMPLEXES = 16
DEV_ROWS = 64
DEVS = 128
F32 = jnp.float32
BF16 = jnp.bfloat16
MESH = pl.DeviceIdType.MESH


def sigmoid(x):
    return 0.5 * jnp.tanh(0.5 * x) + 0.5


def flip(x):
    eye = (
        lax.broadcasted_iota(jnp.int32, (CH, CH), 0) == lax.broadcasted_iota(jnp.int32, (CH, CH), 1)
    ).astype(F32).astype(BF16)
    return lax.dot_general(eye, x, (((1,), (1,)), ((), ())), preferred_element_type=F32)


def norm(x, gain, bias):
    average = jnp.sum(x, axis=0, keepdims=True) * (1.0 / CH)
    centred = x - average
    variance = jnp.sum(centred * centred, axis=0, keepdims=True) * (1.0 / CH)
    return (centred * lax.rsqrt(variance + EPS) * gain + bias).astype(BF16)


def prepare(gain_ref, bias_ref, proj_ref, gate_ref, out_ref, wt, wo, gb):
    for layer in range(2):
        for blk in range(4):
            part = slice(blk * CH, (blk + 1) * CH)
            wt[layer, part] = flip(proj_ref[layer, :, part]).astype(BF16)
        wt[layer, 4 * CH :] = flip(gate_ref[layer]).astype(BF16)
        wo[layer] = flip(out_ref[layer]).astype(BF16)
        for which in range(2):
            for kind, ref in enumerate((gain_ref, bias_ref)):
                line = ref[layer, pl.ds(which, 1), :]
                gb[layer, which, kind] = jnp.transpose(jnp.broadcast_to(line, (CH, CH)))


def project(layer, pair, i, inside, wt, gb, gating, fact):
    gain, bias = gb[layer, 0, 0], gb[layer, 0, 1]
    zn = jnp.concatenate([norm(z, gain, bias) for z in pair], axis=1)
    p = jnp.dot(wt[layer], zn, preferred_element_type=F32)
    for e in range(2):
        q = p[:, e * CH : (e + 1) * CH]
        left = jnp.where(inside, sigmoid(q[:CH]) * q[CH : 2 * CH], 0.0)
        right = jnp.where(inside, sigmoid(q[2 * CH : 3 * CH]) * q[3 * CH : 4 * CH], 0.0)
        fact[0, pl.ds(i + e, CH, stride=HALF), :] = left
        fact[1, pl.ds(i + e, CH, stride=HALF), :] = right
        gating[e] = sigmoid(q[4 * CH :])


def pack(fact, send):
    def step(t, carry):
        for f in range(2):
            block = fact[f, pl.ds(pl.multiple_of(t * 256, 256), 256), :]
            send[f][pl.ds(t * 16, 16)] = block.reshape(16, HALF, CH).astype(BF16)
        return carry

    lax.fori_loop(0, 8, step, 0, unroll=4)


def first_half(half, z_ref, inside, wt, gb, zt, gating, fact, send):
    def step(t, carry):
        i = 2 * t
        row = half * HALF + i
        pair = [flip(z_ref[row + e]) for e in range(2)]
        for e in range(2):
            zt[row + e] = pair[e].astype(BF16)
        project(0, pair, i, inside, wt, gb, gating.at[pl.ds(row, 2)], fact)
        return carry

    lax.fori_loop(0, HALF // 2, step, 0, unroll=4)
    pack(fact, send)


def updated(layer, row, i, inside, wo, gb, zt, gating, sums):
    gain, bias = gb[layer, 1, 0], gb[layer, 1, 1]
    normed = jnp.concatenate(
        [norm(sums[pl.ds(i + e, CH, stride=HALF), :], gain, bias) for e in range(2)], axis=1
    )
    u = jnp.dot(wo[layer], normed, preferred_element_type=F32)
    return [
        jnp.where(
            inside, zt[row + e].astype(F32) + gating[row + e] * u[:, e * CH : (e + 1) * CH], 0.0
        ).astype(BF16)
        for e in range(2)
    ]


def unpack(got, sums):
    def step(t, carry):
        block = got[pl.ds(t * 16, 16)].astype(F32)
        sums[pl.ds(pl.multiple_of(t * 256, 256), 256), :] = block.reshape(256, CH)
        return carry

    lax.fori_loop(0, 8, step, 0, unroll=4)


def middle_half(half, got, inside, wt, wo, gb, zt, gating, sums, fact, send):
    unpack(got, sums)

    def step(t, carry):
        i = 2 * t
        row = half * HALF + i
        pair = updated(0, row, i, inside, wo, gb, zt, gating, sums)
        for e in range(2):
            zt[row + e] = pair[e]
        project(
            1, [z.astype(F32) for z in pair], i, inside, wt, gb, gating.at[pl.ds(row, 2)], fact
        )
        return carry

    lax.fori_loop(0, HALF // 2, step, 0, unroll=4)
    pack(fact, send)


def last_half(half, got, inside, wo, gb, zt, gating, sums, o_ref):
    unpack(got, sums)

    def step(t, carry):
        i = 2 * t
        row = half * HALF + i
        pair = updated(1, row, i, inside, wo, gb, zt, gating, sums)
        for e in range(2):
            o_ref[row + e] = flip(pair[e]).astype(BF16)
        return carry

    lax.fori_loop(0, HALF // 2, step, 0, unroll=4)


def window(ref, begin, count=None, cores=(0, 1)):
    part = ref[pl.ds(2 * begin, 2 * SPAN)].reshape(SPAN, 2, HALF, CH)
    tall = []
    for q in range(SPAN):
        wide = jnp.concatenate([part[q, h] for h in cores], axis=1)
        if count is not None and q >= 2:
            wide = jnp.where(q * ROWS < count, wide, jnp.zeros_like(wide))
        tall.append(wide)
    return jnp.concatenate(tall, axis=0)


def per_complex(begin_ref, count_ref, work):
    def step(b, carry):
        work(b, jnp.clip(begin_ref[b], 0, DEV_ROWS - 1), count_ref[b])
        return carry

    lax.fori_loop(0, COMPLEXES, step, 0, unroll=8)


def keep(block_sums, b, sums):
    for core in range(2):
        block_sums[b, core] = sums[:, core * CH : (core + 1) * CH].astype(BF16).reshape(SPAN, HALF, CH)


def outgoing(begin_ref, count_ref, left, right, block_sums):
    def work(b, begin, count):
        them = jnp.concatenate([window(ref, begin, count) for ref in right], axis=0)
        sums = lax.dot_general(
            window(left, begin), them, (((1,), (1,)), ((), ())), preferred_element_type=F32
        )
        keep(block_sums, b, sums)

    per_complex(begin_ref, count_ref, work)


def incoming_start(begin_ref, count_ref, left, right, partial):
    def work(b, begin, count):
        partial[b] = lax.dot_general(
            window(left, begin),
            window(right, begin, count),
            (((0,), (0,)), ((), ())),
            preferred_element_type=F32,
        )

    per_complex(begin_ref, count_ref, work)


def incoming_end(begin_ref, count_ref, left, right, partial, core, block_sums):
    def work(b, begin, count):
        sums = partial[b, core * CH : (core + 1) * CH] + lax.dot_general(
            window(left, begin, None, (core,)),
            window(right, begin, count),
            (((0,), (0,)), ((), ())),
            preferred_element_type=F32,
        )
        keep(block_sums, b, sums)

    per_complex(begin_ref, count_ref, work)


def spread(begin_ref, block_sums, send):
    def step(r, b):
        later = jnp.minimum(b + 1, COMPLEXES - 1)
        b = jnp.where(begin_ref[later] <= r, later, b)
        q = jnp.clip(r - begin_ref[b], 0, SPAN - 1)
        for core in range(2):
            send[2 * r + core] = block_sums[b, core, q]
        return b

    lax.fori_loop(0, DEV_ROWS, step, jnp.int32(0), unroll=16)


def inside_mask(row, begin_ref, count_ref):
    count = count_ref[0]
    for b in range(1, COMPLEXES):
        count = jnp.where(begin_ref[b] <= row, count_ref[b], count)
    return lax.broadcasted_iota(jnp.int32, (1, CH), 1) * 2 < count


def kernel(
    count_ref, begin_ref, z_hbm, gain_hbm, bias_hbm, proj_hbm, gate_hbm, outw_hbm,
    o_ref,
    z_ref, gain_ref, bias_ref, proj_ref, gate_ref, outw_ref,
    wt, wo, gb, zt, gating, fact, sums, block_sums, partial, load_sem, send_sem, recv_sem, *exchanged,
):
    send, recv, back, got = exchanged[:5], exchanged[5:10], exchanged[10:14], exchanged[14:18]
    row, col = lax.axis_index("row"), lax.axis_index("col")
    me = row * 2 + col
    y, x, z = row >> 4, (row >> 2) & 3, row & 3
    planes = [((y + dy) & 3) * 16 for dy in range(4)]
    cores = (col, 1 - col)

    def peers(work):
        def group(t, first):
            for dy in range(4):
                to = planes[dy] + ((x + (t >> 2) + dy) & 3) * 4 + ((z + t + dy) & 3)
                for core in cores[first:] if dy == 0 else cores:
                    work(to, core)

        def step(t, carry):
            group(t, 0)
            return carry

        group(0, 1)
        lax.fori_loop(1, 16, step, 0)

    loads = [
        pltpu.make_async_copy(src, dst, load_sem.at[k])
        for k, (src, dst) in enumerate(
            (
                (proj_hbm, proj_ref),
                (gate_hbm, gate_ref),
                (outw_hbm, outw_ref),
                (gain_hbm, gain_ref),
                (bias_hbm, bias_ref),
                (z_hbm, z_ref),
            )
        )
    ]
    for load in loads:
        load.start()

    for ref in recv:
        ref[pl.ds(DEVS, 2 * SPAN)] = jnp.zeros((2 * SPAN,) + ref.shape[1:], BF16)

    barrier = pltpu.get_barrier_semaphore()

    peers(
        lambda to, core: pl.semaphore_signal(
            barrier, inc=1, device_id=(to, core), device_id_type=MESH
        )
    )

    inside = inside_mask(row, begin_ref, count_ref)
    for load in loads:
        load.wait()
    prepare(gain_ref, bias_ref, proj_ref, gate_ref, outw_ref, wt, wo, gb)

    def deliver(src, dst, k):
        def copy(to, core):
            pltpu.make_async_remote_copy(
                src_ref=src.at[to * 2 + core],
                dst_ref=dst.at[me],
                send_sem=send_sem.at[k],
                recv_sem=recv_sem.at[k],
                device_id=(to, core),
                device_id_type=MESH,
            ).start()

        peers(copy)

    def others(src, dst, k):
        return pltpu.make_async_remote_copy(
            src_ref=src.at[pl.ds(0, DEVS - 1)],
            dst_ref=dst.at[pl.ds(0, DEVS - 1)],
            send_sem=send_sem.at[k],
            recv_sem=recv_sem.at[k],
            device_id=(row, 1 - col),
            device_id_type=MESH,
        )

    def arrived(src, dst, k):
        others(src, dst, k).wait_recv()
        dst[me] = src[me]

    def forward(k):
        return send[k], recv[k], k

    def backward(k):
        return back[k], got[k], 5 + k

    def factors(refs, k):
        return [refs[k].at[:, f] for f in range(2)]

    def to_back(k):
        spread(begin_ref, block_sums, back[k])
        deliver(*backward(k))

    first_half(0, z_ref, inside, wt, gb, zt, gating, fact, factors(send, 0))
    pl.semaphore_wait(barrier, DEVS - 1)
    deliver(*forward(0))
    first_half(1, z_ref, inside, wt, gb, zt, gating, fact, (send[2], send[1]))
    deliver(*forward(1))
    deliver(*forward(2))

    arrived(*forward(0))
    arrived(*forward(1))
    left, right = factors(recv, 0)
    outgoing(begin_ref, count_ref, left, (right, recv[1]), block_sums)
    to_back(0)
    arrived(*forward(2))
    outgoing(begin_ref, count_ref, recv[2], (right, recv[1]), block_sums)
    to_back(1)

    for half in range(2):
        arrived(*backward(half))
        middle_half(
            half, got[half], inside, wt, wo, gb, zt, gating, sums, fact, factors(send, 3 + half)
        )
        deliver(*forward(3 + half))

    arrived(*forward(3))
    incoming_start(begin_ref, count_ref, *factors(recv, 3), partial)
    arrived(*forward(4))
    for core in range(2):
        incoming_end(begin_ref, count_ref, *factors(recv, 4), partial, core, block_sums)
        to_back(2 + core)

    for half in range(2):
        arrived(*backward(2 + half))
        last_half(half, got[2 + half], inside, wo, gb, zt, gating, sums, o_ref)
    for k in range(5):
        others(*forward(k)).wait_send()
    for k in range(4):
        others(*backward(k)).wait_send()


def body(pair_rep, token_counts, first_device, norm_gain, norm_bias, proj_weight, gate_weight, out_weight):
    smem = pl.BlockSpec(memory_space=pltpu.SMEM)
    anywhere = pl.BlockSpec(memory_space=pl.ANY)
    both, one = (2, HALF, CH), (HALF, CH)
    forms = (both, one, one, both, both)
    loaded = (pair_rep, norm_gain, norm_bias, proj_weight, gate_weight, out_weight)
    return pl.pallas_call(
        kernel,
        out_shape=jax.ShapeDtypeStruct(pair_rep.shape, BF16),
        in_specs=[smem] * 2 + [anywhere] * 6,
        out_specs=pl.BlockSpec(memory_space=pltpu.VMEM),
        scratch_shapes=[pltpu.VMEM(a.shape, a.dtype) for a in loaded]
        + [
            pltpu.VMEM((2, 5 * CH, CH), BF16),
            pltpu.VMEM((2, CH, CH), BF16),
            pltpu.VMEM((2, 2, 2, CH, CH), F32),
            pltpu.VMEM((ROWS, CH, CH), BF16),
            pltpu.VMEM((ROWS, CH, CH), F32),
            pltpu.VMEM((2, CH * HALF, CH), F32),
            pltpu.VMEM((CH * HALF, CH), F32),
            pltpu.VMEM((COMPLEXES, 2, SPAN, HALF, CH), BF16),
            pltpu.VMEM((COMPLEXES, 2 * CH, 2 * CH), F32),
            pltpu.SemaphoreType.DMA((6,)),
            pltpu.SemaphoreType.DMA((9,)),
            pltpu.SemaphoreType.DMA((9,)),
        ]
        + [pltpu.VMEM((DEVS,) + form, BF16) for form in forms]
        + [pltpu.VMEM((DEVS + 2 * SPAN,) + form, BF16) for form in forms]
        + [pltpu.VMEM((DEVS, HALF, CH), BF16)] * 8,
        compiler_params=pltpu.CompilerParams(
            collective_id=0, has_side_effects=True, vmem_limit_bytes=56 * 2**20
        ),
        cost_estimate=pl.CostEstimate(
            flops=3 * 10**9, bytes_accessed=16 * 2**20, transcendentals=6 * 2**20
        ),
    )(token_counts, first_device, *loaded)


def solution(mesh):
    return jax.shard_map(
        body,
        mesh=mesh,
        in_specs=(P("row", "col", None), P(), P(), P(), P(), P(), P(), P()),
        out_specs=P("row", "col", None),
        check_vma=False,
    )
```

```python
import functools

import jax
import jax.numpy as jnp
from jax import lax
from jax.experimental import pallas as pl
from jax.experimental.pallas import tpu as pltpu
from jax.sharding import PartitionSpec as P

EPS = 1e-05
CH = 128
ROWS = 32
HALF = 16
SPAN = 8
COMPLEXES = 16
DEV_ROWS = 64
DEVS = 128
F32 = jnp.float32
BF16 = jnp.bfloat16
MESH = pl.DeviceIdType.MESH


def sigmoid(x):
    return 0.5 * jnp.tanh(0.5 * x) + 0.5


def flip(x):
    eye = (
        lax.broadcasted_iota(jnp.int32, (CH, CH), 0) == lax.broadcasted_iota(jnp.int32, (CH, CH), 1)
    ).astype(F32).astype(BF16)
    return lax.dot_general(eye, x, (((1,), (1,)), ((), ())), preferred_element_type=F32)


def norm(x, gain, bias):
    average = jnp.sum(x, axis=0, keepdims=True) * (1.0 / CH)
    centred = x - average
    variance = jnp.sum(centred * centred, axis=0, keepdims=True) * (1.0 / CH)
    return (centred * lax.rsqrt(variance + EPS) * gain + bias).astype(BF16)


def prepare(gain_ref, bias_ref, proj_ref, gate_ref, out_ref, wt, wo, gb):
    for layer in range(2):
        for blk in range(4):
            part = slice(blk * CH, (blk + 1) * CH)
            wt[layer, part] = flip(proj_ref[layer, :, part]).astype(BF16)
        wt[layer, 4 * CH :] = flip(gate_ref[layer]).astype(BF16)
        wo[layer] = flip(out_ref[layer]).astype(BF16)
        for which in range(2):
            for kind, ref in enumerate((gain_ref, bias_ref)):
                line = ref[layer, pl.ds(which, 1), :]
                gb[layer, which, kind] = jnp.transpose(jnp.broadcast_to(line, (CH, CH)))


def project(layer, pair, i, inside, wt, gb, gating, fact):
    gain, bias = gb[layer, 0, 0], gb[layer, 0, 1]
    zn = jnp.concatenate([norm(z, gain, bias) for z in pair], axis=1)
    p = jnp.dot(wt[layer], zn, preferred_element_type=F32)
    for e in range(2):
        q = p[:, e * CH : (e + 1) * CH]
        left = jnp.where(inside, sigmoid(q[:CH]) * q[CH : 2 * CH], 0.0)
        right = jnp.where(inside, sigmoid(q[2 * CH : 3 * CH]) * q[3 * CH : 4 * CH], 0.0)
        fact[0, pl.ds(i + e, CH, stride=HALF), :] = left
        fact[1, pl.ds(i + e, CH, stride=HALF), :] = right
        gating[e] = sigmoid(q[4 * CH :])


def pack(fact, send):
    def step(t, carry):
        for f in range(2):
            block = fact[f, pl.ds(pl.multiple_of(t * 256, 256), 256), :]
            send[f][pl.ds(t * 16, 16)] = block.reshape(16, HALF, CH).astype(BF16)
        return carry

    lax.fori_loop(0, 8, step, 0, unroll=8)


def first_half(half, z_ref, inside, wt, gb, zt, gating, fact, send):
    def step(t, carry):
        i = 2 * t
        row = half * HALF + i
        pair = [flip(z_ref[row + e]) for e in range(2)]
        for e in range(2):
            zt[row + e] = pair[e].astype(BF16)
        project(0, pair, i, inside, wt, gb, gating.at[pl.ds(row, 2)], fact)
        return carry

    lax.fori_loop(0, HALF // 2, step, 0, unroll=8)
    pack(fact, send)


def updated(layer, row, i, inside, wo, gb, zt, gating, sums):
    gain, bias = gb[layer, 1, 0], gb[layer, 1, 1]
    normed = jnp.concatenate(
        [norm(sums[pl.ds(i + e, CH, stride=HALF), :], gain, bias) for e in range(2)], axis=1
    )
    u = jnp.dot(wo[layer], normed, preferred_element_type=F32)
    return [
        jnp.where(
            inside, zt[row + e].astype(F32) + gating[row + e] * u[:, e * CH : (e + 1) * CH], 0.0
        ).astype(BF16)
        for e in range(2)
    ]


def unpack(got, sums):
    def step(t, carry):
        block = got[pl.ds(t * 16, 16)].astype(F32)
        sums[pl.ds(pl.multiple_of(t * 256, 256), 256), :] = block.reshape(256, CH)
        return carry

    lax.fori_loop(0, 8, step, 0, unroll=8)


def middle_half(half, got, inside, wt, wo, gb, zt, gating, sums, fact, send):
    unpack(got, sums)

    def step(t, carry):
        i = 2 * t
        row = half * HALF + i
        pair = updated(0, row, i, inside, wo, gb, zt, gating, sums)
        for e in range(2):
            zt[row + e] = pair[e]
        project(
            1, [z.astype(F32) for z in pair], i, inside, wt, gb, gating.at[pl.ds(row, 2)], fact
        )
        return carry

    lax.fori_loop(0, HALF // 2, step, 0, unroll=8)
    pack(fact, send)


def last_half(half, got, inside, wo, gb, zt, gating, sums, o_ref):
    unpack(got, sums)

    def step(t, carry):
        i = 2 * t
        row = half * HALF + i
        pair = updated(1, row, i, inside, wo, gb, zt, gating, sums)
        for e in range(2):
            o_ref[row + e] = flip(pair[e]).astype(BF16)
        return carry

    lax.fori_loop(0, HALF // 2, step, 0, unroll=8)


def window(ref, begin, count=None, cores=(0, 1)):
    part = ref[pl.ds(2 * begin, 2 * SPAN)].reshape(SPAN, 2, HALF, CH)
    tall = []
    for q in range(SPAN):
        wide = jnp.concatenate([part[q, h] for h in cores], axis=1)
        if count is not None and q >= 2:
            wide = jnp.where(q * ROWS < count, wide, jnp.zeros_like(wide))
        tall.append(wide)
    return jnp.concatenate(tall, axis=0)


def per_complex(begin_ref, count_ref, work):
    def step(b, carry):
        work(b, jnp.clip(begin_ref[b], 0, DEV_ROWS - 1), count_ref[b])
        return carry

    lax.fori_loop(0, COMPLEXES, step, 0, unroll=8)


def keep(block_sums, b, sums):
    for core in range(2):
        block_sums[b, core] = sums[:, core * CH : (core + 1) * CH].astype(BF16).reshape(SPAN, HALF, CH)


def outgoing(begin_ref, count_ref, left, right, block_sums):
    def work(b, begin, count):
        them = jnp.concatenate([window(ref, begin, count) for ref in right], axis=0)
        sums = lax.dot_general(
            window(left, begin), them, (((1,), (1,)), ((), ())), preferred_element_type=F32
        )
        keep(block_sums, b, sums)

    per_complex(begin_ref, count_ref, work)


def incoming_start(begin_ref, count_ref, left, right, partial):
    def work(b, begin, count):
        partial[b] = lax.dot_general(
            window(left, begin),
            window(right, begin, count),
            (((0,), (0,)), ((), ())),
            preferred_element_type=F32,
        )

    per_complex(begin_ref, count_ref, work)


def incoming_end(begin_ref, count_ref, left, right, partial, core, block_sums):
    def work(b, begin, count):
        sums = partial[b, core * CH : (core + 1) * CH] + lax.dot_general(
            window(left, begin, None, (core,)),
            window(right, begin, count),
            (((0,), (0,)), ((), ())),
            preferred_element_type=F32,
        )
        keep(block_sums, b, sums)

    per_complex(begin_ref, count_ref, work)


def spread(begin_ref, block_sums, send):
    def step(r, b):
        later = jnp.minimum(b + 1, COMPLEXES - 1)
        b = jnp.where(begin_ref[later] <= r, later, b)
        q = jnp.clip(r - begin_ref[b], 0, SPAN - 1)
        for core in range(2):
            send[2 * r + core] = block_sums[b, core, q]
        return b

    lax.fori_loop(0, DEV_ROWS, step, jnp.int32(0), unroll=16)


def inside_mask(row, begin_ref, count_ref):
    count = count_ref[0]
    for b in range(1, COMPLEXES):
        count = jnp.where(begin_ref[b] <= row, count_ref[b], count)
    return lax.broadcasted_iota(jnp.int32, (1, CH), 1) * 2 < count


def kernel(
    count_ref, begin_ref, z_hbm, gain_hbm, bias_hbm, proj_hbm, gate_hbm, outw_hbm,
    o_ref,
    z_ref, gain_ref, bias_ref, proj_ref, gate_ref, outw_ref,
    wt, wo, gb, zt, gating, fact, sums, block_sums, partial, load_sem, send_sem, recv_sem, *exchanged,
):
    send, recv, back, got = exchanged[:5], exchanged[5:10], exchanged[10:14], exchanged[14:18]
    row, col = lax.axis_index("row"), lax.axis_index("col")
    me = row * 2 + col
    y, x, z = row >> 4, (row >> 2) & 3, row & 3
    planes = [((y + dy) & 3) * 16 for dy in range(4)]
    cores = (col, 1 - col)

    def peers(work):
        def group(t, first):
            for dy in range(4):
                to = planes[dy] + ((x + (t >> 2) + dy) & 3) * 4 + ((z + t + dy) & 3)
                for core in cores[first:] if dy == 0 else cores:
                    work(to, core)

        def step(t, carry):
            group(t, 0)
            return carry

        group(0, 1)
        lax.fori_loop(1, 16, step, 0)

    loads = [
        pltpu.make_async_copy(src, dst, load_sem.at[k])
        for k, (src, dst) in enumerate(
            (
                (proj_hbm, proj_ref),
                (gate_hbm, gate_ref),
                (outw_hbm, outw_ref),
                (gain_hbm, gain_ref),
                (bias_hbm, bias_ref),
                (z_hbm, z_ref),
            )
        )
    ]
    for load in loads:
        load.start()

    for ref in recv:
        ref[pl.ds(DEVS, 2 * SPAN)] = jnp.zeros((2 * SPAN,) + ref.shape[1:], BF16)

    barrier = pltpu.get_barrier_semaphore()

    peers(
        lambda to, core: pl.semaphore_signal(
            barrier, inc=1, device_id=(to, core), device_id_type=MESH
        )
    )

    inside = inside_mask(row, begin_ref, count_ref)
    for load in loads:
        load.wait()
    prepare(gain_ref, bias_ref, proj_ref, gate_ref, outw_ref, wt, wo, gb)

    def deliver(src, dst, k):
        def copy(to, core):
            pltpu.make_async_remote_copy(
                src_ref=src.at[to * 2 + core],
                dst_ref=dst.at[me],
                send_sem=send_sem.at[k],
                recv_sem=recv_sem.at[k],
                device_id=(to, core),
                device_id_type=MESH,
            ).start()

        peers(copy)

    def others(src, dst, k):
        return pltpu.make_async_remote_copy(
            src_ref=src.at[pl.ds(0, DEVS - 1)],
            dst_ref=dst.at[pl.ds(0, DEVS - 1)],
            send_sem=send_sem.at[k],
            recv_sem=recv_sem.at[k],
            device_id=(row, 1 - col),
            device_id_type=MESH,
        )

    def arrived(src, dst, k):
        others(src, dst, k).wait_recv()
        dst[me] = src[me]

    def forward(k):
        return send[k], recv[k], k

    def backward(k):
        return back[k], got[k], 5 + k

    def factors(refs, k):
        return [refs[k].at[:, f] for f in range(2)]

    def to_back(k):
        spread(begin_ref, block_sums, back[k])
        deliver(*backward(k))

    first_half(0, z_ref, inside, wt, gb, zt, gating, fact, factors(send, 0))
    pl.semaphore_wait(barrier, DEVS - 1)
    deliver(*forward(0))
    first_half(1, z_ref, inside, wt, gb, zt, gating, fact, (send[2], send[1]))
    deliver(*forward(1))
    deliver(*forward(2))

    arrived(*forward(0))
    arrived(*forward(1))
    left, right = factors(recv, 0)
    outgoing(begin_ref, count_ref, left, (right, recv[1]), block_sums)
    to_back(0)
    arrived(*forward(2))
    outgoing(begin_ref, count_ref, recv[2], (right, recv[1]), block_sums)
    to_back(1)

    for half in range(2):
        arrived(*backward(half))
        middle_half(
            half, got[half], inside, wt, wo, gb, zt, gating, sums, fact, factors(send, 3 + half)
        )
        deliver(*forward(3 + half))

    arrived(*forward(3))
    incoming_start(begin_ref, count_ref, *factors(recv, 3), partial)
    arrived(*forward(4))
    for core in range(2):
        incoming_end(begin_ref, count_ref, *factors(recv, 4), partial, core, block_sums)
        to_back(2 + core)

    for half in range(2):
        arrived(*backward(2 + half))
        last_half(half, got[2 + half], inside, wo, gb, zt, gating, sums, o_ref)
    for k in range(5):
        others(*forward(k)).wait_send()
    for k in range(4):
        others(*backward(k)).wait_send()


def body(pair_rep, token_counts, first_device, norm_gain, norm_bias, proj_weight, gate_weight, out_weight):
    smem = pl.BlockSpec(memory_space=pltpu.SMEM)
    anywhere = pl.BlockSpec(memory_space=pl.ANY)
    both, one = (2, HALF, CH), (HALF, CH)
    forms = (both, one, one, both, both)
    loaded = (pair_rep, norm_gain, norm_bias, proj_weight, gate_weight, out_weight)
    return pl.pallas_call(
        kernel,
        out_shape=jax.ShapeDtypeStruct(pair_rep.shape, BF16),
        in_specs=[smem] * 2 + [anywhere] * 6,
        out_specs=pl.BlockSpec(memory_space=pltpu.VMEM),
        scratch_shapes=[pltpu.VMEM(a.shape, a.dtype) for a in loaded]
        + [
            pltpu.VMEM((2, 5 * CH, CH), BF16),
            pltpu.VMEM((2, CH, CH), BF16),
            pltpu.VMEM((2, 2, 2, CH, CH), F32),
            pltpu.VMEM((ROWS, CH, CH), BF16),
            pltpu.VMEM((ROWS, CH, CH), F32),
            pltpu.VMEM((2, CH * HALF, CH), F32),
            pltpu.VMEM((CH * HALF, CH), F32),
            pltpu.VMEM((COMPLEXES, 2, SPAN, HALF, CH), BF16),
            pltpu.VMEM((COMPLEXES, 2 * CH, 2 * CH), F32),
            pltpu.SemaphoreType.DMA((6,)),
            pltpu.SemaphoreType.DMA((9,)),
            pltpu.SemaphoreType.DMA((9,)),
        ]
        + [pltpu.VMEM((DEVS,) + form, BF16) for form in forms]
        + [pltpu.VMEM((DEVS + 2 * SPAN,) + form, BF16) for form in forms]
        + [pltpu.VMEM((DEVS, HALF, CH), BF16)] * 8,
        compiler_params=pltpu.CompilerParams(
            collective_id=0, has_side_effects=True, vmem_limit_bytes=56 * 2**20
        ),
        cost_estimate=pl.CostEstimate(
            flops=3 * 10**9, bytes_accessed=16 * 2**20, transcendentals=6 * 2**20
        ),
    )(token_counts, first_device, *loaded)


def solution(mesh):
    return jax.shard_map(
        body,
        mesh=mesh,
        in_specs=(P("row", "col", None), P(), P(), P(), P(), P(), P(), P()),
        out_specs=P("row", "col", None),
        check_vma=False,
    )
```

```python
import functools

import jax
import jax.numpy as jnp
from jax import lax
from jax.experimental import pallas as pl
from jax.experimental.pallas import tpu as pltpu
from jax.sharding import PartitionSpec as P

EPS = 1e-05
CH = 128
ROWS = 32
HALF = 16
SPAN = 8
COMPLEXES = 16
DEV_ROWS = 64
DEVS = 128
F32 = jnp.float32
BF16 = jnp.bfloat16
MESH = pl.DeviceIdType.MESH


def sigmoid(x):
    return 0.5 * jnp.tanh(0.5 * x) + 0.5


def flip(x):
    eye = (
        lax.broadcasted_iota(jnp.int32, (CH, CH), 0) == lax.broadcasted_iota(jnp.int32, (CH, CH), 1)
    ).astype(F32).astype(BF16)
    return lax.dot_general(eye, x, (((1,), (1,)), ((), ())), preferred_element_type=F32)


def norm(x, gain, bias):
    average = jnp.sum(x, axis=0, keepdims=True) * (1.0 / CH)
    centred = x - average
    variance = jnp.sum(centred * centred, axis=0, keepdims=True) * (1.0 / CH)
    return (centred * lax.rsqrt(variance + EPS) * gain + bias).astype(BF16)


def prepare(gain_ref, bias_ref, proj_ref, gate_ref, out_ref, wt, wo, gb):
    for layer in range(2):
        for blk in range(4):
            part = slice(blk * CH, (blk + 1) * CH)
            wt[layer, part] = flip(proj_ref[layer, :, part]).astype(BF16)
        wt[layer, 4 * CH :] = flip(gate_ref[layer]).astype(BF16)
        wo[layer] = flip(out_ref[layer]).astype(BF16)
        for which in range(2):
            for kind, ref in enumerate((gain_ref, bias_ref)):
                line = ref[layer, pl.ds(which, 1), :]
                gb[layer, which, kind] = jnp.transpose(jnp.broadcast_to(line, (CH, CH)))


def project(layer, pair, i, inside, wt, gb, gating, fact):
    gain, bias = gb[layer, 0, 0], gb[layer, 0, 1]
    zn = jnp.concatenate([norm(z, gain, bias) for z in pair], axis=1)
    p = jnp.dot(wt[layer], zn, preferred_element_type=F32)
    for e in range(2):
        q = p[:, e * CH : (e + 1) * CH]
        left = jnp.where(inside, sigmoid(q[:CH]) * q[CH : 2 * CH], 0.0)
        right = jnp.where(inside, sigmoid(q[2 * CH : 3 * CH]) * q[3 * CH : 4 * CH], 0.0)
        fact[0, pl.ds(i + e, CH, stride=HALF), :] = left
        fact[1, pl.ds(i + e, CH, stride=HALF), :] = right
        gating[e] = sigmoid(q[4 * CH :])


def pack(fact, send):
    def step(t, carry):
        for f in range(2):
            block = fact[f, pl.ds(pl.multiple_of(t * 256, 256), 256), :]
            send[f][pl.ds(t * 16, 16)] = block.reshape(16, HALF, CH).astype(BF16)
        return carry

    lax.fori_loop(0, 8, step, 0, unroll=8)


def first_half(half, z_ref, inside, wt, gb, zt, gating, fact, send):
    def step(t, carry):
        i = 2 * t
        row = half * HALF + i
        pair = [flip(z_ref[row + e]) for e in range(2)]
        for e in range(2):
            zt[row + e] = pair[e].astype(BF16)
        project(0, pair, i, inside, wt, gb, gating.at[pl.ds(row, 2)], fact)
        return carry

    lax.fori_loop(0, HALF // 2, step, 0, unroll=8)
    pack(fact, send)


def updated(layer, row, i, inside, wo, gb, zt, gating, sums):
    gain, bias = gb[layer, 1, 0], gb[layer, 1, 1]
    normed = jnp.concatenate(
        [norm(sums[pl.ds(i + e, CH, stride=HALF), :], gain, bias) for e in range(2)], axis=1
    )
    u = jnp.dot(wo[layer], normed, preferred_element_type=F32)
    return [
        jnp.where(
            inside, zt[row + e].astype(F32) + gating[row + e] * u[:, e * CH : (e + 1) * CH], 0.0
        ).astype(BF16)
        for e in range(2)
    ]


def unpack(got, sums):
    def step(t, carry):
        block = got[pl.ds(t * 16, 16)].astype(F32)
        sums[pl.ds(pl.multiple_of(t * 256, 256), 256), :] = block.reshape(256, CH)
        return carry

    lax.fori_loop(0, 8, step, 0, unroll=8)


def middle_half(half, got, inside, wt, wo, gb, zt, gating, sums, fact, send):
    unpack(got, sums)

    def step(t, carry):
        i = 2 * t
        row = half * HALF + i
        pair = updated(0, row, i, inside, wo, gb, zt, gating, sums)
        for e in range(2):
            zt[row + e] = pair[e]
        project(
            1, [z.astype(F32) for z in pair], i, inside, wt, gb, gating.at[pl.ds(row, 2)], fact
        )
        return carry

    lax.fori_loop(0, HALF // 2, step, 0, unroll=8)
    pack(fact, send)


def last_half(half, got, inside, wo, gb, zt, gating, sums, o_ref):
    unpack(got, sums)

    def step(t, carry):
        i = 2 * t
        row = half * HALF + i
        pair = updated(1, row, i, inside, wo, gb, zt, gating, sums)
        for e in range(2):
            o_ref[row + e] = flip(pair[e]).astype(BF16)
        return carry

    lax.fori_loop(0, HALF // 2, step, 0, unroll=8)


def window(ref, begin, count=None, cores=(0, 1)):
    part = ref[pl.ds(2 * begin, 2 * SPAN)].reshape(SPAN, 2, HALF, CH)
    tall = []
    for q in range(SPAN):
        wide = jnp.concatenate([part[q, h] for h in cores], axis=1)
        if count is not None and q >= 2:
            wide = jnp.where(q * ROWS < count, wide, jnp.zeros_like(wide))
        tall.append(wide)
    return jnp.concatenate(tall, axis=0)


def per_complex(begin_ref, count_ref, work):
    def step(b, carry):
        work(b, jnp.clip(begin_ref[b], 0, DEV_ROWS - 1), count_ref[b])
        return carry

    lax.fori_loop(0, COMPLEXES, step, 0, unroll=8)


def keep(block_sums, b, sums):
    for core in range(2):
        block_sums[b, core] = sums[:, core * CH : (core + 1) * CH].astype(BF16).reshape(SPAN, HALF, CH)


def outgoing(begin_ref, count_ref, left, right, block_sums):
    def work(b, begin, count):
        them = jnp.concatenate([window(ref, begin, count) for ref in right], axis=0)
        sums = lax.dot_general(
            window(left, begin), them, (((1,), (1,)), ((), ())), preferred_element_type=F32
        )
        keep(block_sums, b, sums)

    per_complex(begin_ref, count_ref, work)


def incoming_start(begin_ref, count_ref, left, right, partial):
    def work(b, begin, count):
        partial[b] = lax.dot_general(
            window(left, begin),
            window(right, begin, count),
            (((0,), (0,)), ((), ())),
            preferred_element_type=F32,
        )

    per_complex(begin_ref, count_ref, work)


def incoming_end(begin_ref, count_ref, left, right, partial, core, block_sums):
    def work(b, begin, count):
        sums = partial[b, core * CH : (core + 1) * CH] + lax.dot_general(
            window(left, begin, None, (core,)),
            window(right, begin, count),
            (((0,), (0,)), ((), ())),
            preferred_element_type=F32,
        )
        keep(block_sums, b, sums)

    per_complex(begin_ref, count_ref, work)


def spread(begin_ref, block_sums, send):
    def step(r, b):
        later = jnp.minimum(b + 1, COMPLEXES - 1)
        b = jnp.where(begin_ref[later] <= r, later, b)
        q = jnp.clip(r - begin_ref[b], 0, SPAN - 1)
        for core in range(2):
            send[2 * r + core] = block_sums[b, core, q]
        return b

    lax.fori_loop(0, DEV_ROWS, step, jnp.int32(0), unroll=16)


def inside_mask(row, begin_ref, count_ref):
    count = count_ref[0]
    for b in range(1, COMPLEXES):
        count = jnp.where(begin_ref[b] <= row, count_ref[b], count)
    return lax.broadcasted_iota(jnp.int32, (1, CH), 1) * 2 < count


def kernel(
    count_ref, begin_ref, z_hbm, gain_hbm, bias_hbm, proj_hbm, gate_hbm, outw_hbm,
    o_ref,
    z_ref, gain_ref, bias_ref, proj_ref, gate_ref, outw_ref,
    wt, wo, gb, zt, gating, fact, sums, block_sums, partial, load_sem, send_sem, recv_sem, *exchanged,
):
    send, recv, back, got = exchanged[:5], exchanged[5:10], exchanged[10:14], exchanged[14:18]
    row, col = lax.axis_index("row"), lax.axis_index("col")
    me = row * 2 + col
    y, x, z = row >> 4, (row >> 2) & 3, row & 3
    planes = [((y + dy) & 3) * 16 for dy in range(4)]
    cores = (col, 1 - col)

    def peers(work):
        def group(t, first):
            for dy in range(4):
                to = planes[dy] + ((x + (t >> 2) + dy) & 3) * 4 + ((z + t + dy) & 3)
                for core in cores[first:] if dy == 0 else cores:
                    work(to, core)

        def step(t, carry):
            group(t, 0)
            return carry

        group(0, 1)
        lax.fori_loop(1, 16, step, 0)

    loads = [
        pltpu.make_async_copy(src, dst, load_sem.at[k])
        for k, (src, dst) in enumerate(
            (
                (proj_hbm, proj_ref),
                (gate_hbm, gate_ref),
                (outw_hbm, outw_ref),
                (gain_hbm, gain_ref),
                (bias_hbm, bias_ref),
                (z_hbm, z_ref),
            )
        )
    ]
    for load in loads:
        load.start()

    for ref in recv:
        ref[pl.ds(DEVS, 2 * SPAN)] = jnp.zeros((2 * SPAN,) + ref.shape[1:], BF16)

    barrier = pltpu.get_barrier_semaphore()

    peers(
        lambda to, core: pl.semaphore_signal(
            barrier, inc=1, device_id=(to, core), device_id_type=MESH
        )
    )

    inside = inside_mask(row, begin_ref, count_ref)
    for load in loads:
        load.wait()
    prepare(gain_ref, bias_ref, proj_ref, gate_ref, outw_ref, wt, wo, gb)

    def deliver(src, dst, k):
        def copy(to, core):
            pltpu.make_async_remote_copy(
                src_ref=src.at[to * 2 + core],
                dst_ref=dst.at[me],
                send_sem=send_sem.at[k],
                recv_sem=recv_sem.at[k],
                device_id=(to, core),
                device_id_type=MESH,
            ).start()

        peers(copy)

    def others(src, dst, k):
        return pltpu.make_async_remote_copy(
            src_ref=src.at[pl.ds(0, DEVS - 1)],
            dst_ref=dst.at[pl.ds(0, DEVS - 1)],
            send_sem=send_sem.at[k],
            recv_sem=recv_sem.at[k],
            device_id=(row, 1 - col),
            device_id_type=MESH,
        )

    def arrived(src, dst, k):
        others(src, dst, k).wait_recv()
        dst[me] = src[me]

    def forward(k):
        return send[k], recv[k], k

    def backward(k):
        return back[k], got[k], 5 + k

    def factors(refs, k):
        return [refs[k].at[:, f] for f in range(2)]

    def to_back(k):
        spread(begin_ref, block_sums, back[k])
        deliver(*backward(k))

    first_half(0, z_ref, inside, wt, gb, zt, gating, fact, factors(send, 0))
    pl.semaphore_wait(barrier, DEVS - 1)
    deliver(*forward(0))
    first_half(1, z_ref, inside, wt, gb, zt, gating, fact, (send[2], send[1]))
    deliver(*forward(1))
    deliver(*forward(2))

    arrived(*forward(0))
    arrived(*forward(1))
    left, right = factors(recv, 0)
    outgoing(begin_ref, count_ref, left, (right, recv[1]), block_sums)
    to_back(0)
    arrived(*forward(2))
    outgoing(begin_ref, count_ref, recv[2], (right, recv[1]), block_sums)
    to_back(1)

    for half in range(2):
        arrived(*backward(half))
        middle_half(
            half, got[half], inside, wt, wo, gb, zt, gating, sums, fact, factors(send, 3 + half)
        )
        deliver(*forward(3 + half))

    arrived(*forward(3))
    incoming_start(begin_ref, count_ref, *factors(recv, 3), partial)
    arrived(*forward(4))
    for core in range(2):
        incoming_end(begin_ref, count_ref, *factors(recv, 4), partial, core, block_sums)
        to_back(2 + core)

    for half in range(2):
        arrived(*backward(2 + half))
        last_half(half, got[2 + half], inside, wo, gb, zt, gating, sums, o_ref)
    for k in range(5):
        others(*forward(k)).wait_send()
    for k in range(4):
        others(*backward(k)).wait_send()


def body(pair_rep, token_counts, first_device, norm_gain, norm_bias, proj_weight, gate_weight, out_weight):
    smem = pl.BlockSpec(memory_space=pltpu.SMEM)
    anywhere = pl.BlockSpec(memory_space=pl.ANY)
    both, one = (2, HALF, CH), (HALF, CH)
    forms = (both, one, one, both, both)
    loaded = (pair_rep, norm_gain, norm_bias, proj_weight, gate_weight, out_weight)
    return pl.pallas_call(
        kernel,
        out_shape=jax.ShapeDtypeStruct(pair_rep.shape, BF16),
        in_specs=[smem] * 2 + [anywhere] * 6,
        out_specs=pl.BlockSpec(memory_space=pltpu.VMEM),
        scratch_shapes=[pltpu.VMEM(a.shape, a.dtype) for a in loaded]
        + [
            pltpu.VMEM((2, 5 * CH, CH), BF16),
            pltpu.VMEM((2, CH, CH), BF16),
            pltpu.VMEM((2, 2, 2, CH, CH), F32),
            pltpu.VMEM((ROWS, CH, CH), BF16),
            pltpu.VMEM((ROWS, CH, CH), F32),
            pltpu.VMEM((2, CH * HALF + HALF, CH), F32),
            pltpu.VMEM((CH * HALF + HALF, CH), F32),
            pltpu.VMEM((COMPLEXES, 2, SPAN, HALF, CH), BF16),
            pltpu.VMEM((COMPLEXES, 2 * CH, 2 * CH), F32),
            pltpu.SemaphoreType.DMA((6,)),
            pltpu.SemaphoreType.DMA((9,)),
            pltpu.SemaphoreType.DMA((9,)),
        ]
        + [pltpu.VMEM((DEVS,) + form, BF16) for form in forms]
        + [pltpu.VMEM((DEVS + 2 * SPAN,) + form, BF16) for form in forms]
        + [pltpu.VMEM((DEVS, HALF, CH), BF16)] * 8,
        compiler_params=pltpu.CompilerParams(
            collective_id=0, has_side_effects=True, vmem_limit_bytes=56 * 2**20
        ),
        cost_estimate=pl.CostEstimate(
            flops=3 * 10**9, bytes_accessed=16 * 2**20, transcendentals=6 * 2**20
        ),
    )(token_counts, first_device, *loaded)


def solution(mesh):
    return jax.shard_map(
        body,
        mesh=mesh,
        in_specs=(P("row", "col", None), P(), P(), P(), P(), P(), P(), P()),
        out_specs=P("row", "col", None),
        check_vma=False,
    )
```

```python
import functools

import jax
import jax.numpy as jnp
from jax import lax
from jax.experimental import pallas as pl
from jax.experimental.pallas import tpu as pltpu
from jax.sharding import PartitionSpec as P

EPS = 1e-05
CH = 128
ROWS = 32
HALF = 16
SPAN = 8
COMPLEXES = 16
DEV_ROWS = 64
DEVS = 128
F32 = jnp.float32
BF16 = jnp.bfloat16
MESH = pl.DeviceIdType.MESH


def sigmoid(x):
    return 0.5 * jnp.tanh(0.5 * x) + 0.5


def flip(x):
    eye = (
        lax.broadcasted_iota(jnp.int32, (CH, CH), 0) == lax.broadcasted_iota(jnp.int32, (CH, CH), 1)
    ).astype(F32).astype(BF16)
    return lax.dot_general(eye, x, (((1,), (1,)), ((), ())), preferred_element_type=F32)


def norm(x, gain, bias):
    average = jnp.sum(x, axis=0, keepdims=True) * (1.0 / CH)
    centred = x - average
    variance = jnp.sum(centred * centred, axis=0, keepdims=True) * (1.0 / CH)
    return (centred * lax.rsqrt(variance + EPS) * gain + bias).astype(BF16)


def prepare(gain_ref, bias_ref, proj_ref, gate_ref, out_ref, wt, wo, gb):
    for layer in range(2):
        for blk in range(4):
            part = slice(blk * CH, (blk + 1) * CH)
            wt[layer, part] = flip(proj_ref[layer, :, part]).astype(BF16)
        wt[layer, 4 * CH :] = flip(gate_ref[layer]).astype(BF16)
        wo[layer] = flip(out_ref[layer]).astype(BF16)
        for which in range(2):
            for kind, ref in enumerate((gain_ref, bias_ref)):
                line = ref[layer, pl.ds(which, 1), :]
                gb[layer, which, kind] = jnp.transpose(jnp.broadcast_to(line, (CH, CH)))


def project(layer, pair, i, inside, wt, gb, gating, fact):
    gain, bias = gb[layer, 0, 0], gb[layer, 0, 1]
    zn = jnp.concatenate([norm(z, gain, bias) for z in pair], axis=1)
    p = jnp.dot(wt[layer], zn, preferred_element_type=F32)
    for e in range(2):
        q = p[:, e * CH : (e + 1) * CH]
        left = jnp.where(inside, sigmoid(q[:CH]) * q[CH : 2 * CH], 0.0)
        right = jnp.where(inside, sigmoid(q[2 * CH : 3 * CH]) * q[3 * CH : 4 * CH], 0.0)
        fact[0, pl.ds(i + e, CH, stride=HALF), :] = left
        fact[1, pl.ds(i + e, CH, stride=HALF), :] = right
        gating[e] = sigmoid(q[4 * CH :])


def pack(fact, send):
    def step(t, carry):
        for f in range(2):
            block = fact[f, pl.ds(pl.multiple_of(t * 256, 256), 256), :]
            send[f][pl.ds(t * 16, 16)] = block.reshape(16, HALF, CH).astype(BF16)
        return carry

    lax.fori_loop(0, 8, step, 0, unroll=8)


def first_half(half, z_ref, inside, wt, gb, zt, gating, fact, send):
    def step(t, carry):
        i = 2 * t
        row = half * HALF + i
        pair = [flip(z_ref[row + e]) for e in range(2)]
        for e in range(2):
            zt[row + e] = pair[e].astype(BF16)
        project(0, pair, i, inside, wt, gb, gating.at[pl.ds(row, 2)], fact)
        return carry

    lax.fori_loop(0, HALF // 2, step, 0, unroll=8)
    pack(fact, send)


def updated(layer, row, i, inside, wo, gb, zt, gating, sums):
    gain, bias = gb[layer, 1, 0], gb[layer, 1, 1]
    normed = jnp.concatenate(
        [norm(sums[pl.ds(i + e, CH, stride=HALF), :], gain, bias) for e in range(2)], axis=1
    )
    u = jnp.dot(wo[layer], normed, preferred_element_type=F32)
    return [
        jnp.where(
            inside, zt[row + e].astype(F32) + gating[row + e] * u[:, e * CH : (e + 1) * CH], 0.0
        ).astype(BF16)
        for e in range(2)
    ]


def unpack(got, sums):
    def step(t, carry):
        block = got[pl.ds(t * 16, 16)].astype(F32)
        sums[pl.ds(pl.multiple_of(t * 256, 256), 256), :] = block.reshape(256, CH)
        return carry

    lax.fori_loop(0, 8, step, 0, unroll=8)


def middle_half(half, got, inside, wt, wo, gb, zt, gating, sums, fact, send):
    unpack(got, sums)

    def step(t, carry):
        i = 2 * t
        row = half * HALF + i
        pair = updated(0, row, i, inside, wo, gb, zt, gating, sums)
        for e in range(2):
            zt[row + e] = pair[e]
        project(
            1, [z.astype(F32) for z in pair], i, inside, wt, gb, gating.at[pl.ds(row, 2)], fact
        )
        return carry

    lax.fori_loop(0, HALF // 2, step, 0, unroll=8)
    pack(fact, send)


def last_half(half, got, inside, wo, gb, zt, gating, sums, o_ref):
    unpack(got, sums)

    def step(t, carry):
        i = 2 * t
        row = half * HALF + i
        pair = updated(1, row, i, inside, wo, gb, zt, gating, sums)
        for e in range(2):
            o_ref[row + e] = flip(pair[e]).astype(BF16)
        return carry

    lax.fori_loop(0, HALF // 2, step, 0, unroll=8)


def window(ref, begin, count=None, cores=(0, 1)):
    part = ref[pl.ds(2 * begin, 2 * SPAN)].reshape(SPAN, 2, HALF, CH)
    tall = []
    for q in range(SPAN):
        wide = jnp.concatenate([part[q, h] for h in cores], axis=1)
        if count is not None and q >= 2:
            wide = jnp.where(q * ROWS < count, wide, jnp.zeros_like(wide))
        tall.append(wide)
    return jnp.concatenate(tall, axis=0)


def per_complex(begin_ref, count_ref, work):
    def step(b, carry):
        work(b, jnp.clip(begin_ref[b], 0, DEV_ROWS - 1), count_ref[b])
        return carry

    lax.fori_loop(0, COMPLEXES, step, 0, unroll=8)


def keep(block_sums, b, sums):
    for core in range(2):
        block_sums[b, core] = sums[:, core * CH : (core + 1) * CH].astype(BF16).reshape(SPAN, HALF, CH)


def outgoing(begin_ref, count_ref, left, right, block_sums):
    def work(b, begin, count):
        them = jnp.concatenate([window(ref, begin, count) for ref in right], axis=0)
        sums = lax.dot_general(
            window(left, begin), them, (((1,), (1,)), ((), ())), preferred_element_type=F32
        )
        keep(block_sums, b, sums)

    per_complex(begin_ref, count_ref, work)


def incoming_start(begin_ref, count_ref, left, right, partial):
    def work(b, begin, count):
        partial[b] = lax.dot_general(
            window(left, begin),
            window(right, begin, count),
            (((0,), (0,)), ((), ())),
            preferred_element_type=F32,
        )

    per_complex(begin_ref, count_ref, work)


def incoming_end(begin_ref, count_ref, left, right, partial, core, block_sums):
    def work(b, begin, count):
        sums = partial[b, core * CH : (core + 1) * CH] + lax.dot_general(
            window(left, begin, None, (core,)),
            window(right, begin, count),
            (((0,), (0,)), ((), ())),
            preferred_element_type=F32,
        )
        keep(block_sums, b, sums)

    per_complex(begin_ref, count_ref, work)


def spread(begin_ref, block_sums, send):
    def step(r, b):
        later = jnp.minimum(b + 1, COMPLEXES - 1)
        b = jnp.where(begin_ref[later] <= r, later, b)
        q = jnp.clip(r - begin_ref[b], 0, SPAN - 1)
        for core in range(2):
            send[2 * r + core] = block_sums[b, core, q]
        return b

    lax.fori_loop(0, DEV_ROWS, step, jnp.int32(0), unroll=16)


def inside_mask(row, begin_ref, count_ref):
    count = count_ref[0]
    for b in range(1, COMPLEXES):
        count = jnp.where(begin_ref[b] <= row, count_ref[b], count)
    return lax.broadcasted_iota(jnp.int32, (1, CH), 1) * 2 < count


def kernel(
    count_ref, begin_ref, z_hbm, gain_hbm, bias_hbm, proj_hbm, gate_hbm, outw_hbm,
    o_ref,
    z_ref, gain_ref, bias_ref, proj_ref, gate_ref, outw_ref,
    wt, wo, gb, zt, gating, fact, sums, block_sums, partial, load_sem, send_sem, recv_sem, *exchanged,
):
    send, recv, back, got = exchanged[:5], exchanged[5:10], exchanged[10:14], exchanged[14:18]
    row, col = lax.axis_index("row"), lax.axis_index("col")
    me = row * 2 + col
    y, x, z = row >> 4, (row >> 2) & 3, row & 3
    planes = [((y + dy) & 3) * 16 for dy in range(4)]
    cores = (col, 1 - col)

    def peers(work):
        def group(t, first):
            for dy in range(4):
                to = planes[dy] + ((x + (t >> 2) + dy) & 3) * 4 + ((z + t + dy) & 3)
                for core in cores[first:] if dy == 0 else cores:
                    work(to, core)

        def step(t, carry):
            group(t, 0)
            return carry

        group(0, 1)
        lax.fori_loop(1, 16, step, 0, unroll=3)

    loads = [
        pltpu.make_async_copy(src, dst, load_sem.at[k])
        for k, (src, dst) in enumerate(
            (
                (proj_hbm, proj_ref),
                (gate_hbm, gate_ref),
                (outw_hbm, outw_ref),
                (gain_hbm, gain_ref),
                (bias_hbm, bias_ref),
                (z_hbm, z_ref),
            )
        )
    ]
    for load in loads:
        load.start()

    for ref in recv:
        ref[pl.ds(DEVS, 2 * SPAN)] = jnp.zeros((2 * SPAN,) + ref.shape[1:], BF16)

    barrier = pltpu.get_barrier_semaphore()

    peers(
        lambda to, core: pl.semaphore_signal(
            barrier, inc=1, device_id=(to, core), device_id_type=MESH
        )
    )

    inside = inside_mask(row, begin_ref, count_ref)
    for load in loads:
        load.wait()
    prepare(gain_ref, bias_ref, proj_ref, gate_ref, outw_ref, wt, wo, gb)

    def deliver(src, dst, k):
        def copy(to, core):
            pltpu.make_async_remote_copy(
                src_ref=src.at[to * 2 + core],
                dst_ref=dst.at[me],
                send_sem=send_sem.at[k],
                recv_sem=recv_sem.at[k],
                device_id=(to, core),
                device_id_type=MESH,
            ).start()

        peers(copy)

    def others(src, dst, k):
        return pltpu.make_async_remote_copy(
            src_ref=src.at[pl.ds(0, DEVS - 1)],
            dst_ref=dst.at[pl.ds(0, DEVS - 1)],
            send_sem=send_sem.at[k],
            recv_sem=recv_sem.at[k],
            device_id=(row, 1 - col),
            device_id_type=MESH,
        )

    def arrived(src, dst, k):
        others(src, dst, k).wait_recv()
        dst[me] = src[me]

    def forward(k):
        return send[k], recv[k], k

    def backward(k):
        return back[k], got[k], 5 + k

    def factors(refs, k):
        return [refs[k].at[:, f] for f in range(2)]

    def to_back(k):
        spread(begin_ref, block_sums, back[k])
        deliver(*backward(k))

    first_half(0, z_ref, inside, wt, gb, zt, gating, fact, factors(send, 0))
    pl.semaphore_wait(barrier, DEVS - 1)
    deliver(*forward(0))
    first_half(1, z_ref, inside, wt, gb, zt, gating, fact, (send[2], send[1]))
    deliver(*forward(1))
    deliver(*forward(2))

    arrived(*forward(0))
    arrived(*forward(1))
    left, right = factors(recv, 0)
    outgoing(begin_ref, count_ref, left, (right, recv[1]), block_sums)
    to_back(0)
    arrived(*forward(2))
    outgoing(begin_ref, count_ref, recv[2], (right, recv[1]), block_sums)
    to_back(1)

    for half in range(2):
        arrived(*backward(half))
        middle_half(
            half, got[half], inside, wt, wo, gb, zt, gating, sums, fact, factors(send, 3 + half)
        )
        deliver(*forward(3 + half))

    arrived(*forward(3))
    incoming_start(begin_ref, count_ref, *factors(recv, 3), partial)
    arrived(*forward(4))
    for core in range(2):
        incoming_end(begin_ref, count_ref, *factors(recv, 4), partial, core, block_sums)
        to_back(2 + core)

    for half in range(2):
        arrived(*backward(2 + half))
        last_half(half, got[2 + half], inside, wo, gb, zt, gating, sums, o_ref)
    for k in range(5):
        others(*forward(k)).wait_send()
    for k in range(4):
        others(*backward(k)).wait_send()


def body(pair_rep, token_counts, first_device, norm_gain, norm_bias, proj_weight, gate_weight, out_weight):
    smem = pl.BlockSpec(memory_space=pltpu.SMEM)
    anywhere = pl.BlockSpec(memory_space=pl.ANY)
    both, one = (2, HALF, CH), (HALF, CH)
    forms = (both, one, one, both, both)
    loaded = (pair_rep, norm_gain, norm_bias, proj_weight, gate_weight, out_weight)
    return pl.pallas_call(
        kernel,
        out_shape=jax.ShapeDtypeStruct(pair_rep.shape, BF16),
        in_specs=[smem] * 2 + [anywhere] * 6,
        out_specs=pl.BlockSpec(memory_space=pltpu.VMEM),
        scratch_shapes=[pltpu.VMEM(a.shape, a.dtype) for a in loaded]
        + [
            pltpu.VMEM((2, 5 * CH, CH), BF16),
            pltpu.VMEM((2, CH, CH), BF16),
            pltpu.VMEM((2, 2, 2, CH, CH), F32),
            pltpu.VMEM((ROWS, CH, CH), BF16),
            pltpu.VMEM((ROWS, CH, CH), F32),
            pltpu.VMEM((2, CH * HALF + HALF, CH), F32),
            pltpu.VMEM((CH * HALF + HALF, CH), F32),
            pltpu.VMEM((COMPLEXES, 2, SPAN, HALF, CH), BF16),
            pltpu.VMEM((COMPLEXES, 2 * CH, 2 * CH), F32),
            pltpu.SemaphoreType.DMA((6,)),
            pltpu.SemaphoreType.DMA((9,)),
            pltpu.SemaphoreType.DMA((9,)),
        ]
        + [pltpu.VMEM((DEVS,) + form, BF16) for form in forms]
        + [pltpu.VMEM((DEVS + 2 * SPAN,) + form, BF16) for form in forms]
        + [pltpu.VMEM((DEVS, HALF, CH), BF16)] * 8,
        compiler_params=pltpu.CompilerParams(
            collective_id=0, has_side_effects=True, vmem_limit_bytes=56 * 2**20
        ),
        cost_estimate=pl.CostEstimate(
            flops=3 * 10**9, bytes_accessed=16 * 2**20, transcendentals=6 * 2**20
        ),
    )(token_counts, first_device, *loaded)


def solution(mesh):
    return jax.shard_map(
        body,
        mesh=mesh,
        in_specs=(P("row", "col", None), P(), P(), P(), P(), P(), P(), P()),
        out_specs=P("row", "col", None),
        check_vma=False,
    )
```
